32 devices in a mesh: shard: 8 (over y, x, core), rep: 4 (over z).
Axes of the slice: x: 2, y: 2, z: 4, core: 2. Of those that a mesh axis runs over, the one named last changes fastest.
Arguments:
- tokens: bfloat16 [32768, 768], P(('shard', 'rep')), may hold values from -6 to 6
- segments: int32 [32768], P(('shard', 'rep')), may hold values from -1 to 1023, as said below
- cotangent: bfloat16 [32768, 768], P(('shard', 'rep')), may hold values from -6 to 6
- attend_gain: bfloat16 [768], P('shard'), may hold values from 0.099609375 to 1.8984375
- attend_shift: bfloat16 [768], P('shard'), may hold values from -2 to 2
- triple_weight: bfloat16 [768, 2304], P('shard'), may hold values from -0.21875 to 0.21875
- triple_bias: bfloat16 [1536], P('shard'), may hold values from -2 to 2
- output_weight: bfloat16 [768, 768], P('shard'), may hold values from -0.875 to 0.875
- output_bias: bfloat16 [768], P('shard'), may hold values from -2 to 2
- feed_gain: bfloat16 [768], P('shard'), may hold values from 0.099609375 to 1.8984375
- feed_shift: bfloat16 [768], P('shard'), may hold values from -2 to 2
- expand_weight: bfloat16 [768, 3072], P('shard'), may hold values from -0.21875 to 0.21875
- expand_bias: bfloat16 [3072], P('shard'), may hold values from -2 to 2
- reduce_weight: bfloat16 [3072, 768], P('shard'), may hold values from -0.109375 to 0.109375
- reduce_bias: bfloat16 [768], P('shard'), may hold values from -2 to 2
Outputs:
- out_tokens: bfloat16 [32768, 768], P(('shard', 'rep'))
- grad_tokens: bfloat16 [32768, 768], P(('shard', 'rep'))
- grad_attend_gain: float32 [768], P('shard')
- grad_attend_shift: float32 [768], P('shard')
- grad_triple_weight: float32 [768, 2304], P('shard')
- grad_triple_bias: float32 [1536], P('shard')
- grad_output_weight: float32 [768, 768], P('shard')
- grad_output_bias: float32 [768], P('shard')
- grad_feed_gain: float32 [768], P('shard')
- grad_feed_shift: float32 [768], P('shard')
- grad_expand_weight: float32 [768, 3072], P('shard')
- grad_expand_bias: float32 [3072], P('shard')
- grad_reduce_weight: float32 [3072, 768], P('shard')
- grad_reduce_bias: float32 [768], P('shard')
The draws below stay inside these ranges and needn't reach their ends.
Inputs may be any that keep to these rules, and one draw needn't show every extreme that they name: `segments`: within the 1024 slots of one device, numbers never fall along the slots, start at 0 and rise by at most one from slot to slot; empty slots (-1) come after all live slots of that device; each document has at most 1024 tokens; some device holds a single document of 1024 tokens, some device holds 1024 documents of one token, and some device has empty slots; every device has 256 live slots or more.
All inputs are finite; a program needn't handle non-finite values.
Results may differ from the reference program's by a relative error of at most 0.018.
Values may be sent and summed in bfloat16 or wider, within the bound.
No kernel may reach another device: no remote copies, remote signals or barrier semaphores. Data moves between devices by JAX's collectives and lax.ppermute only.
A program may use at most 256 MiB of HBM per device.

```python
import jax
import jax.numpy as jnp
from jax import lax

D = 768
HEADS = 12
HEAD_DIM = 64
FF = 3072
TOK_DEV = 1024
TOKENS = 32768


def draw_segments(key, part):
    key = jax.random.fold_in(key, 11)
    device_count = TOKENS // TOK_DEV
    first_key, second_key, third_key = jax.random.split(key, 3)
    levels = jax.random.randint(first_key, (device_count,), 0, 3)
    chosen = jax.random.randint(second_key, (), 0, device_count)
    device_ids = jnp.arange(device_count)
    levels = jnp.where(device_ids == chosen, 0, levels)
    levels = jnp.where(device_ids == (chosen + 1) % device_count, 1, levels)
    levels = jnp.where(device_ids == (chosen + 2) % device_count, 2, levels)
    levels = jnp.where(device_ids == (chosen + 3) % device_count, 0, levels)
    live_count = jnp.right_shift(jnp.full((device_count,), TOK_DEV, jnp.int32), levels.astype(jnp.int32))
    positions = jnp.arange(TOK_DEV)[None, :]
    starts = jax.random.randint(third_key, (device_count, TOK_DEV), 0, 64) == 0
    starts = starts | (positions == 0)
    starts = jnp.where((device_ids == chosen)[:, None], positions == 0, starts)
    starts = jnp.where((device_ids == (chosen + 3) % device_count)[:, None], positions >= 0, starts)
    numbers = jnp.cumsum(starts.astype(jnp.int32), axis=1) - 1
    numbers = jnp.where(positions < live_count[:, None], numbers, -1)
    return numbers.reshape(-1).astype(jnp.int32)


def block_levels(rng, dims, pieces, low, high):
    def one(axis_at, parts):
        steps = jax.random.uniform(jax.random.fold_in(jax.random.fold_in(rng, 6), axis_at), (parts,), jnp.float32, low / len(pieces), high / len(pieces))
        return jnp.repeat(jnp.exp(steps), dims[axis_at] // parts).reshape((-1,) + (1,) * (len(dims) - axis_at - 1))

    level = one(*pieces[0])
    for cut in pieces[1:]:
        level = level * one(*cut)
    return level


def centred(own_key, dims, scale, bound, cuts=(), dtype=jnp.bfloat16):
    level = block_levels(own_key, dims, cuts, -0.22, 0.18) if cuts else 1.0
    entries = jax.random.normal(own_key, dims, jnp.float32) * scale * level
    return jnp.minimum(jnp.maximum(entries, -bound), bound).astype(dtype)


def setup_inputs(seed: int = 0) -> dict:
    arg_keys = jax.random.split(jax.random.key(seed), 16)
    tokens = centred(arg_keys[0], (TOKENS, D), 1.0, 6.0, ((0, 32),))
    segments = draw_segments(jax.random.fold_in(arg_keys[15], 71), 0)
    cotangent = centred(arg_keys[2], (TOKENS, D), 1.0, 6.0, ((0, 32),))
    attend_gain = jnp.clip(1.0 + 0.18 * jax.random.normal(arg_keys[3], (D,), jnp.float32), 0.099609375, 1.8984375).astype(jnp.bfloat16)
    attend_shift = centred(arg_keys[4], (D,), 0.3, 2.0, ((0, 8),))
    triple_weight = centred(arg_keys[5], (D, 3 * D), D ** -0.5, 0.21875, ((0, 8),))
    triple_bias = centred(arg_keys[6], (2 * D,), 0.3, 2.0, ((0, 8),))
    output_weight = centred(arg_keys[7], (D, D), (D // 16) ** -0.5, 0.875, ((0, 8),))
    output_bias = centred(arg_keys[8], (D,), 0.3, 2.0, ((0, 8),))
    feed_gain = jnp.clip(1.0 + 0.18 * jax.random.normal(arg_keys[9], (D,), jnp.float32), 0.099609375, 1.8984375).astype(jnp.bfloat16)
    feed_shift = centred(arg_keys[10], (D,), 0.3, 2.0, ((0, 8),))
    expand_weight = centred(arg_keys[11], (D, FF), D ** -0.5, 0.21875, ((0, 8),))
    expand_bias = centred(arg_keys[12], (FF,), 0.3, 2.0, ((0, 8),))
    reduce_weight = centred(arg_keys[13], (FF, D), FF ** -0.5, 0.109375, ((0, 8),))
    reduce_bias = centred(arg_keys[14], (D,), 0.3, 2.0, ((0, 8),))
    return {"tokens": tokens, "segments": segments, "cotangent": cotangent, "attend_gain": attend_gain, "attend_shift": attend_shift, "triple_weight": triple_weight, "triple_bias": triple_bias, "output_weight": output_weight, "output_bias": output_bias, "feed_gain": feed_gain, "feed_shift": feed_shift, "expand_weight": expand_weight, "expand_bias": expand_bias, "reduce_weight": reduce_weight, "reduce_bias": reduce_bias}


@jax.custom_vjp
def low(v):
    return lax.optimization_barrier(v.astype(jnp.bfloat16)).astype(jnp.float32)

@jax.custom_vjp
def low_back(v):
    return v

def low_keep(v):
    return (low(v), None)

def low_pass(kept, grad):
    return (grad,)

def back_keep(v):
    return (v, None)

def back_low(kept, grad):
    return (low(grad),)
low.defvjp(low_keep, low_pass)
low_back.defvjp(back_keep, back_low)
epsilon = 1e-05

def layer_norm(values, gain, shift):
    center = values - lax.optimization_barrier(jnp.mean(values, axis=-1, keepdims=True))
    variance = lax.optimization_barrier(jnp.mean(center * center, axis=-1, keepdims=True))
    return center * lax.rsqrt(variance + epsilon) * gain + shift

def matmul(left, right):
    return jnp.dot(left, right, precision=lax.Precision.HIGHEST, preferred_element_type=jnp.float32)

def forward(inputs, segments, params):
    attend_gain, attend_shift, triple_weight, triple_bias, output_weight, output_bias, feed_gain, feed_shift, expand_weight, expand_bias, reduce_weight, reduce_bias = params
    rows = inputs.shape[0]
    normed = low(layer_norm(inputs, attend_gain, attend_shift))
    bias_full = jnp.concatenate([triple_bias[:D], jnp.zeros((D,), jnp.float32), triple_bias[D:]])
    projected = low_back(low(matmul(normed, triple_weight) + bias_full))
    queries = projected[:, :D].reshape(rows, HEADS, HEAD_DIM)
    keys = projected[:, D:2 * D].reshape(rows, HEADS, HEAD_DIM)
    values = projected[:, 2 * D:].reshape(rows, HEADS, HEAD_DIM)
    scores = jnp.einsum('qhd,khd->hqk', queries, keys, precision=lax.Precision.HIGHEST) * 0.125
    scores = low_back(scores)
    positions = jnp.arange(rows)
    allowed = (segments[:, None] == segments[None, :]) & (positions[None, :] <= positions[:, None])
    masked = jnp.where(allowed[None], scores, -1000000000.0)
    probs = low(jax.nn.softmax(masked, axis=-1))
    mixed = jnp.einsum('hqk,khd->qhd', probs, values, precision=lax.Precision.HIGHEST).reshape(rows, D)
    mixed = low_back(low(mixed))
    branch = low_back(matmul(mixed, output_weight) + output_bias)
    middle = inputs + branch
    normed_two = low(layer_norm(middle, feed_gain, feed_shift))
    expanded = low_back(matmul(normed_two, expand_weight) + expand_bias)
    hidden = low(jax.nn.gelu(expanded))
    feed = low_back(matmul(hidden, reduce_weight) + reduce_bias)
    live_rows = (segments >= 0).astype(jnp.float32)[:, None]
    return live_rows * (middle + feed)

def reference(tokens, segments, cotangent, attend_gain, attend_shift, triple_weight, triple_bias, output_weight, output_bias, feed_gain, feed_shift, expand_weight, expand_bias, reduce_weight, reduce_bias):
    params = tuple((item.astype(jnp.float32) for item in (attend_gain, attend_shift, triple_weight, triple_bias, output_weight, output_bias, feed_gain, feed_shift, expand_weight, expand_bias, reduce_weight, reduce_bias)))
    blocks = TOKENS // TOK_DEV
    inputs = tokens.astype(jnp.float32).reshape(blocks, TOK_DEV, D)
    seg_blocks = segments.reshape(blocks, TOK_DEV)
    cot_blocks = cotangent.astype(jnp.float32).reshape(blocks, TOK_DEV, D)

    def step(totals, item):
        block_in, block_seg, block_cot = item
        result, pullback = jax.vjp(lambda first, second: forward(first, block_seg, second), block_in, params)
        grad_in, grad_params = pullback(block_cot)
        totals = jax.tree.map(lambda left, right: left + right, totals, grad_params)
        return (totals, (result.astype(jnp.bfloat16), grad_in.astype(jnp.bfloat16)))
    zeros = jax.tree.map(jnp.zeros_like, params)
    totals, (outputs, grads) = lax.scan(step, zeros, (inputs, seg_blocks, cot_blocks))
    return (outputs.reshape(TOKENS, D), grads.reshape(TOKENS, D), totals[0], totals[1], totals[2], totals[3], totals[4], totals[5], totals[6], totals[7], totals[8], totals[9], totals[10], totals[11])
```

```python
import functools

import jax
import jax.numpy as jnp
from jax import lax
from jax.experimental import pallas as pl
from jax.experimental.pallas import tpu as pltpu
from jax.sharding import PartitionSpec as P

HEAD_DIM = 64
PARTS = 8
CHUNKS = 3
EPSILON = 1e-05
BF = jnp.bfloat16
F32 = jnp.float32
NEVER = -1e30
ROOT = 0.7978845608028654
MIB = 1 << 20


def dot_nn(left, right):
    return lax.dot_general(left, right, (((1,), (0,)), ((), ())), preferred_element_type=F32)


def dot_nt(left, right):
    return lax.dot_general(left, right, (((1,), (1,)), ((), ())), preferred_element_type=F32)


def dot_tn(left, right):
    return lax.dot_general(left, right, (((0,), (0,)), ((), ())), preferred_element_type=F32)


def normalise(values):
    center = values - jnp.mean(values, axis=-1, keepdims=True)
    variance = jnp.mean(center * center, axis=-1, keepdims=True)
    scale = lax.rsqrt(variance + EPSILON)
    return center * scale, scale


def norm_back(values, incoming, gain):
    unit, scale = normalise(values)
    scaled = incoming * gain
    first = jnp.mean(scaled, axis=-1, keepdims=True)
    second = jnp.mean(scaled * unit, axis=-1, keepdims=True)
    back = scale * (scaled - first - unit * second)
    return back, jnp.sum(incoming * unit, axis=0, keepdims=True)


def whole_spec(shape):
    return pl.BlockSpec(shape, lambda *_: (0,) * len(shape))


def params(mib):
    return pltpu.CompilerParams(vmem_limit_bytes=mib * MIB)


def cost(flops, moved, exps=0):
    return pl.CostEstimate(flops=int(flops), bytes_accessed=int(moved), transcendentals=int(exps))


def fill_weight(order_ref, pack_ref, first, blocks, out_ref, rows, lead=None):
    mine = order_ref[0]
    for part in range(PARTS):
        piece = part ^ mine
        for at in range(blocks):
            tile = pack_ref[piece, first + at * rows : first + (at + 1) * rows, :]
            if lead is None:
                out_ref[part * rows : (part + 1) * rows, at * 128 : (at + 1) * 128] = tile
            else:
                group, inside = divmod(at, lead)
                out_ref[group, part * rows : (part + 1) * rows, inside * 128 : (inside + 1) * 128] = tile


def project_kernel(width, order_ref, pack_ref, x_ref, gain_ref, shift_ref, bias_ref, qkv_ref, turned_ref, w_ref):
    @pl.when(pl.program_id(0) == 0)
    def _():
        fill_weight(order_ref, pack_ref, 0, 3 * width // 128, w_ref, width // PARTS, width // 128)

    unit, _ = normalise(x_ref[...].astype(F32))
    normed = (unit * gain_ref[...] + shift_ref[...]).astype(BF)
    turned_ref[...] = normed.T
    for at in range(3):
        qkv_ref[at] = (dot_nn(normed, w_ref[at]) + bias_ref[at]).astype(BF)


def project(order, pack, x, gain, shift, bias):
    rows, width = x.shape
    block = min(256, rows)
    return pl.pallas_call(
        functools.partial(project_kernel, width),
        grid_spec=pltpu.PrefetchScalarGridSpec(
            num_scalar_prefetch=1,
            grid=(rows // block,),
            in_specs=[
                whole_spec(pack.shape),
                pl.BlockSpec((block, width), lambda i, *_: (i, 0)),
                whole_spec(gain.shape),
                whole_spec(shift.shape),
                whole_spec(bias.shape),
            ],
            out_specs=[
                pl.BlockSpec((3, block, width), lambda i, *_: (0, i, 0)),
                pl.BlockSpec((width, block), lambda i, *_: (0, i)),
            ],
            scratch_shapes=[pltpu.VMEM((3, width, width), BF)],
        ),
        out_shape=[
            jax.ShapeDtypeStruct((3, rows, width), BF),
            jax.ShapeDtypeStruct((width, rows), BF),
        ],
        compiler_params=params(40),
        cost_estimate=cost(6 * rows * width * width, 14 * rows * width),
        name="project",
    )(order, pack, x, gain, shift, bias)


def attend_forward_kernel(block, col_ref, row_ref, qkv_ref, mixed_ref, log_ref, bias_ref):
    rows = row_ref.shape[1]

    @pl.when(pl.program_id(0) == 0)
    def _():
        for first in range(0, rows, block):
            at = lax.broadcasted_iota(jnp.int32, (block, rows), 0) + first
            key = lax.broadcasted_iota(jnp.int32, (block, rows), 1)
            same = col_ref[first : first + block, :] == row_ref[...]
            bias_ref[first : first + block, :] = jnp.where(same & (key <= at), 0.0, NEVER)

    lane = lax.broadcasted_iota(jnp.int32, (block, 128), 1)
    for first in range(0, rows, block):
        last = first + block
        queries = qkv_ref[0, first:last, :] * jnp.asarray(0.125, BF)
        outs, logs = [], []
        for head in range(2):
            mine = (lane < HEAD_DIM) if head == 0 else (lane >= HEAD_DIM)
            scores = dot_nt(jnp.where(mine, queries, jnp.zeros_like(queries)), qkv_ref[1, :last, :])
            scores = scores + bias_ref[first:last, :last]
            largest = jnp.max(scores, axis=-1, keepdims=True)
            expo = jnp.exp(scores - largest)
            total = jnp.sum(expo, axis=-1, keepdims=True)
            outs.append(dot_nn(expo.astype(BF), qkv_ref[2, :last, :]) / total)
            logs.append(largest + jnp.log(total))
        mixed_ref[first:last, :] = jnp.where(lane < HEAD_DIM, outs[0], outs[1]).astype(BF)
        log_ref[0, first:last, :] = jnp.where(lane < HEAD_DIM, logs[1], logs[0])


def attend_forward(col, row, qkv):
    _, rows, width = qkv.shape
    pairs = width // 128
    block = min(256, rows)
    return pl.pallas_call(
        functools.partial(attend_forward_kernel, block),
        grid=(pairs,),
        in_specs=[
            whole_spec(col.shape),
            whole_spec(row.shape),
            pl.BlockSpec((3, rows, 128), lambda i: (0, 0, i)),
        ],
        out_specs=[
            pl.BlockSpec((rows, 128), lambda i: (0, i)),
            pl.BlockSpec((1, rows, 128), lambda i: (i, 0, 0)),
        ],
        scratch_shapes=[pltpu.VMEM((rows, rows), F32)],
        out_shape=[
            jax.ShapeDtypeStruct((rows, width), BF),
            jax.ShapeDtypeStruct((pairs, rows, 128), F32),
        ],
        compiler_params=params(32),
        cost_estimate=cost(16 * rows * rows * width, 12 * rows * width, rows * rows * pairs),
        name="attend_forward",
    )(col, row, qkv)


def split_lanes(value, lane):
    high = value.astype(BF)
    rest = value - high.astype(F32)
    middle = rest.astype(BF)
    low = (rest - middle.astype(F32)).astype(BF)
    inside = lax.rem(lane, HEAD_DIM)
    zero = jnp.zeros_like(high)
    return jnp.where(inside == 0, high, jnp.where(inside == 1, middle, jnp.where(inside == 2, low, zero)))


def attend_backward_kernel(
    block, col_ref, row_ref, qkv_ref, mixed_ref, log_ref, grad_ref, out_ref, bias_ref, q_ref, k_ref, d_ref, v_ref, dq_ref
):
    rows = row_ref.shape[1]

    @pl.when(pl.program_id(0) == 0)
    def _():
        for first in range(0, rows, block):
            key = lax.broadcasted_iota(jnp.int32, (block, rows), 0) + first
            at = lax.broadcasted_iota(jnp.int32, (block, rows), 1)
            same = col_ref[first : first + block, :] == row_ref[...]
            bias_ref[first : first + block, :] = jnp.where(same & (key <= at), 0.0, NEVER)

    lane = lax.broadcasted_iota(jnp.int32, (block, 128), 1)
    below = lane < HEAD_DIM
    minus = jnp.where(lax.rem(lane, HEAD_DIM) < 3, -1.0, 0.0).astype(BF)
    for first in range(0, rows, block):
        last = first + block
        queries = qkv_ref[0, first:last, :] * jnp.asarray(0.125, BF)
        keys = qkv_ref[1, first:last, :]
        values = qkv_ref[2, first:last, :]
        grads = grad_ref[first:last, :]
        product = grads.astype(F32) * mixed_ref[first:last, :].astype(F32)
        sums = [
            jnp.sum(jnp.where(below, product, 0.0), axis=-1, keepdims=True),
            jnp.sum(jnp.where(below, 0.0, product), axis=-1, keepdims=True),
        ]
        logs = split_lanes(log_ref[0, first:last, :], lane)
        inner = split_lanes(jnp.where(below, sums[1], sums[0]), lane)
        for head in range(2):
            mine = below if head == 0 else lane >= HEAD_DIM
            q_ref[head, first:last, :] = jnp.where(mine, queries, logs)
            k_ref[head, first:last, :] = jnp.where(mine, keys, minus)
            d_ref[head, first:last, :] = jnp.where(mine, grads, inner)
            v_ref[head, first:last, :] = jnp.where(mine, values, minus)

    for first in range(0, rows, block):
        last = first + block
        key_parts, value_parts, query_parts = [], [], []
        for head in range(2):
            scores = dot_nt(k_ref[head, first:last, :], q_ref[head, first:, :]) + bias_ref[first:last, first:]
            probs = jnp.exp(scores)
            slopes = probs * dot_nt(v_ref[head, first:last, :], d_ref[head, first:, :])
            slopes = slopes.astype(BF)
            value_parts.append(dot_nn(probs.astype(BF), d_ref[head, first:, :]))
            key_parts.append(dot_nn(slopes, q_ref[head, first:, :]))
            query_parts.append(dot_tn(slopes, k_ref[head, first:last, :]))
        out_ref[1, first:last, :] = jnp.where(below, key_parts[0], key_parts[1]).astype(BF)
        out_ref[2, first:last, :] = jnp.where(below, value_parts[0], value_parts[1]).astype(BF)
        side = lax.broadcasted_iota(jnp.int32, (rows - first, 128), 1) < HEAD_DIM
        part = jnp.where(side, query_parts[0], query_parts[1])
        if first == 0:
            dq_ref[...] = part
        else:
            dq_ref[first:, :] += part
    out_ref[0] = (dq_ref[...] * 0.125).astype(BF)


def attend_backward(col, row, qkv, mixed, log_total, grad):
    _, rows, width = qkv.shape
    pairs = width // 128
    block = min(256, rows)
    return pl.pallas_call(
        functools.partial(attend_backward_kernel, block),
        grid=(pairs,),
        in_specs=[
            whole_spec(col.shape),
            whole_spec(row.shape),
            pl.BlockSpec((3, rows, 128), lambda i: (0, 0, i)),
            pl.BlockSpec((rows, 128), lambda i: (0, i)),
            pl.BlockSpec((1, rows, 128), lambda i: (i, 0, 0)),
            pl.BlockSpec((rows, 128), lambda i: (0, i)),
        ],
        out_specs=pl.BlockSpec((3, rows, 128), lambda i: (0, 0, i)),
        scratch_shapes=[pltpu.VMEM((rows, rows), F32)]
        + [pltpu.VMEM((2, rows, 128), BF)] * 4
        + [pltpu.VMEM((rows, 128), F32)],
        out_shape=jax.ShapeDtypeStruct((3, rows, width), BF),
        compiler_params=params(40),
        cost_estimate=cost(40 * rows * rows * width, 20 * rows * width, rows * rows * pairs),
        name="attend_backward",
    )(col, row, qkv, mixed, log_total, grad)


def middle_kernel(
    width, order_ref, pack_ref, x_ref, mixed_ref, seg_ref, cot_ref, bias_ref, gain_ref, shift_ref,
    middle_ref, normed_ref, turned_ref, feed_ref, w_ref
):
    @pl.when(pl.program_id(0) == 0)
    def _():
        fill_weight(order_ref, pack_ref, 0, width // 128, w_ref, width // PARTS)

    middle = x_ref[...].astype(F32) + dot_nn(mixed_ref[...], w_ref[...]) + bias_ref[...]
    middle_ref[...] = middle
    unit, _ = normalise(middle)
    normed = (unit * gain_ref[...] + shift_ref[...]).astype(BF)
    normed_ref[...] = normed
    turned_ref[...] = normed.T
    live = seg_ref[...] >= 0
    feed_ref[...] = jnp.where(live, cot_ref[...].astype(F32), 0.0).astype(BF)


def make_middle(order, pack, x, mixed, col, cot, bias, gain, shift):
    rows, width = x.shape
    block = min(256, rows)
    by_rows = pl.BlockSpec((block, width), lambda i, *_: (i, 0))
    return pl.pallas_call(
        functools.partial(middle_kernel, width),
        grid_spec=pltpu.PrefetchScalarGridSpec(
            num_scalar_prefetch=1,
            grid=(rows // block,),
            in_specs=[
                whole_spec(pack.shape),
                by_rows,
                by_rows,
                pl.BlockSpec((block, 1), lambda i, *_: (i, 0)),
                by_rows,
                whole_spec(bias.shape),
                whole_spec(gain.shape),
                whole_spec(shift.shape),
            ],
            out_specs=[by_rows, by_rows, pl.BlockSpec((width, block), lambda i, *_: (0, i)), by_rows],
            scratch_shapes=[pltpu.VMEM((width, width), BF)],
        ),
        out_shape=[
            jax.ShapeDtypeStruct((rows, width), F32),
            jax.ShapeDtypeStruct((rows, width), BF),
            jax.ShapeDtypeStruct((width, rows), BF),
            jax.ShapeDtypeStruct((rows, width), BF),
        ],
        compiler_params=params(32),
        cost_estimate=cost(2 * rows * width * width, 16 * rows * width),
        name="middle",
    )(order, pack, x, mixed, col, cot, bias, gain, shift)


def feed_kernel(
    width, hidden, steps, has_sum, order_ref, pack_ref, normed_ref, turned_ref, feed_ref, bias_ref, *refs
):
    if has_sum:
        out_in_ref, back_in_ref, *refs = refs
    out_ref, back_ref, grad_ref, sum_ref, we_ref, wr_ref, h_ref, e_ref = refs
    step = pl.program_id(0)
    block = normed_ref.shape[0]
    share = width // PARTS
    mine = order_ref[0]

    @pl.when(step == 0)
    def _():
        fill_weight(order_ref, pack_ref, 0, hidden // 128, we_ref, share)
        fill_weight(order_ref, pack_ref, hidden // 128 * share, width // 128, wr_ref, hidden // PARTS)

    @pl.when(step < steps)
    def _():
        here = pl.ds(pl.multiple_of(step * block, block), block)
        normed = normed_ref[...]
        feed = feed_ref[here, :]
        for at in range(0, hidden, 256):
            cols = slice(at, at + 256)
            u = dot_nn(normed, we_ref[:, cols]) + bias_ref[:, cols]
            hidden_grad = dot_nt(feed, wr_ref[cols, :])
            square = u * u
            tanh = jnp.tanh(ROOT * u * (1.0 + 0.044715 * square))
            half = 0.5 + 0.5 * tanh
            h_ref[here, cols] = (u * half).astype(BF)
            slope = half + (0.5 * ROOT) * u * (1.0 - tanh * tanh) * (1.0 + (3 * 0.044715) * square)
            e_ref[here, cols] = (hidden_grad * slope).astype(BF)
        out = dot_nn(h_ref[here, :], wr_ref[...])
        back = dot_nt(e_ref[here, :], we_ref[...])
        if has_sum:
            out = out + out_in_ref[...]
            back = back + back_in_ref[...]
        out_ref[...] = out
        back_ref[...] = back

    @pl.when(step >= steps)
    def _():
        at = step - steps
        cols = pl.ds(pl.multiple_of(at * 256, 256), 256)
        e_part = e_ref[:, cols]
        sum_ref[:, cols] = jnp.sum(e_part.astype(F32), axis=0, keepdims=True)
        grad = dot_nn(turned_ref[...], e_part).astype(BF)
        for side in range(2):
            base = pl.multiple_of((2 * at + side) * share, share)
            for part in range(PARTS):
                grad_ref[part ^ mine, pl.ds(base, share), :] = grad[
                    part * share : (part + 1) * share, side * 128 : (side + 1) * 128
                ]
        grad = dot_tn(h_ref[:, cols], feed_ref[...]).astype(BF)
        first = hidden // 128 * share
        for side in range(2):
            part = (2 * at + side) ^ mine
            for lane in range(width // 128):
                grad_ref[part, first + lane * 128 : first + (lane + 1) * 128, :] = grad[
                    side * 128 : (side + 1) * 128, lane * 128 : (lane + 1) * 128
                ]


def feed_chunk(order, pack, normed, turned, feed, bias, sums):
    rows, width = normed.shape
    hidden = bias.shape[1]
    block = min(256, rows)
    steps = rows // block
    by_rows = pl.BlockSpec((block, width), lambda i, *_: (jnp.minimum(i, steps - 1), 0))
    return pl.pallas_call(
        functools.partial(feed_kernel, width, hidden, steps, bool(sums)),
        grid_spec=pltpu.PrefetchScalarGridSpec(
            num_scalar_prefetch=1,
            grid=(steps + hidden // 256,),
            in_specs=[
                whole_spec(pack.shape),
                by_rows,
                whole_spec(turned.shape),
                whole_spec(feed.shape),
                whole_spec(bias.shape),
            ]
            + [by_rows] * len(sums),
            out_specs=[by_rows, by_rows, whole_spec(pack.shape), whole_spec((1, hidden))],
            scratch_shapes=[
                pltpu.VMEM((width, hidden), BF),
                pltpu.VMEM((hidden, width), BF),
                pltpu.VMEM((rows, hidden), BF),
                pltpu.VMEM((rows, hidden), BF),
            ],
        ),
        out_shape=[
            jax.ShapeDtypeStruct((rows, width), F32),
            jax.ShapeDtypeStruct((rows, width), F32),
            jax.ShapeDtypeStruct(pack.shape, BF),
            jax.ShapeDtypeStruct((1, hidden), F32),
        ],
        compiler_params=params(48),
        cost_estimate=cost(12 * rows * width * hidden, 20 * rows * width, rows * hidden),
        name="feed",
    )(order, pack, normed, turned, feed, bias, *sums)


def branch_kernel(
    width, steps, order_ref, pack_ref, back_ref, middle_ref, sum_ref, feed_ref, seg_ref, mixed_ref, gain_ref, bias_ref,
    out_ref, grad_ref, mixed_grad_ref, pack_grad_ref, sums_ref, w_ref, b_ref, t_ref
):
    step = pl.program_id(0)
    block = back_ref.shape[0]
    share = width // PARTS
    mine = order_ref[0]

    @pl.when(step == 0)
    def _():
        fill_weight(order_ref, pack_ref, 0, width // 128, w_ref, share)
        sums_ref[...] = jnp.zeros_like(sums_ref)

    middle = middle_ref[...]
    live = seg_ref[...] >= 0
    out_ref[...] = jnp.where(live, middle + sum_ref[...] + bias_ref[...], 0.0).astype(BF)
    back = back_ref[...]
    feed = feed_ref[...].astype(F32)
    part, gain_sum = norm_back(middle, back, gain_ref[...])
    grad = feed + part
    grad_ref[...] = grad
    branch = grad.astype(BF)
    b_ref[pl.ds(pl.multiple_of(step * block, block), block), :] = branch
    mixed_grad_ref[...] = dot_nt(branch, w_ref[...]).astype(BF)
    sums_ref[0:1, :] += gain_sum
    sums_ref[1:2, :] += jnp.sum(back, axis=0, keepdims=True)
    sums_ref[2:3, :] += jnp.sum(branch.astype(F32), axis=0, keepdims=True)
    sums_ref[3:4, :] += jnp.sum(feed, axis=0, keepdims=True)

    @pl.when(step == steps - 1)
    def _():
        for first in range(0, width, 256):
            t_ref[first : first + 256, :] = dot_tn(mixed_ref[:, first : first + 256], b_ref[...]).astype(BF)
        for part in range(PARTS):
            for lane in range(width // 128):
                pack_grad_ref[part ^ mine, lane * share : (lane + 1) * share, :] = t_ref[
                    part * share : (part + 1) * share, lane * 128 : (lane + 1) * 128
                ]


def branch(order, pack, back, middle, total, feed, col, mixed, gain, bias):
    rows, width = middle.shape
    block = min(256, rows)
    steps = rows // block
    by_rows = pl.BlockSpec((block, width), lambda i, *_: (i, 0))
    return pl.pallas_call(
        functools.partial(branch_kernel, width, steps),
        grid_spec=pltpu.PrefetchScalarGridSpec(
            num_scalar_prefetch=1,
            grid=(steps,),
            in_specs=[
                whole_spec(pack.shape),
                by_rows,
                by_rows,
                by_rows,
                by_rows,
                pl.BlockSpec((block, 1), lambda i, *_: (i, 0)),
                whole_spec(mixed.shape),
                whole_spec(gain.shape),
                whole_spec(bias.shape),
            ],
            out_specs=[by_rows, by_rows, by_rows, whole_spec(pack.shape), whole_spec((8, width))],
            scratch_shapes=[
                pltpu.VMEM((width, width), BF),
                pltpu.VMEM((rows, width), BF),
                pltpu.VMEM((width, width), BF),
            ],
        ),
        out_shape=[
            jax.ShapeDtypeStruct((rows, width), BF),
            jax.ShapeDtypeStruct((rows, width), F32),
            jax.ShapeDtypeStruct((rows, width), BF),
            jax.ShapeDtypeStruct(pack.shape, BF),
            jax.ShapeDtypeStruct((8, width), F32),
        ],
        compiler_params=params(40),
        cost_estimate=cost(4 * rows * width * width, 24 * rows * width),
        name="branch",
    )(order, pack, back, middle, total, feed, col, mixed, gain, bias)


def triple_kernel(width, order_ref, turned_ref, grad_ref, pack_ref, sum_ref):
    share = width // PARTS
    mine = order_ref[0]
    grads = grad_ref[0]
    sum_ref[...] = jnp.sum(grads.astype(F32), axis=0, keepdims=True)
    product = dot_nn(turned_ref[...], grads).astype(BF)
    for side in range(2):
        for part in range(PARTS):
            pack_ref[part ^ mine, side * share : (side + 1) * share, :] = product[
                part * share : (part + 1) * share, side * 128 : (side + 1) * 128
            ]


def triple_grad(order, turned, grads):
    width, rows = turned.shape
    share = width // PARTS
    per = width // 256
    return pl.pallas_call(
        functools.partial(triple_kernel, width),
        grid_spec=pltpu.PrefetchScalarGridSpec(
            num_scalar_prefetch=1,
            grid=(3 * per,),
            in_specs=[
                whole_spec(turned.shape),
                pl.BlockSpec((1, rows, 256), lambda i, *_: (i // per, 0, i % per)),
            ],
            out_specs=[
                pl.BlockSpec((PARTS, 2 * share, 128), lambda i, *_: (0, i, 0)),
                pl.BlockSpec((1, 256), lambda i, *_: (0, i)),
            ],
        ),
        out_shape=[
            jax.ShapeDtypeStruct((PARTS, 3 * width // 128 * share, 128), BF),
            jax.ShapeDtypeStruct((1, 3 * width), F32),
        ],
        compiler_params=params(32),
        cost_estimate=cost(6 * rows * width * width, 12 * rows * width),
        name="triple_grad",
    )(order, turned, grads)


def input_kernel(width, order_ref, pack_ref, x_ref, grads_ref, middle_ref, gain_ref, out_ref, sums_ref, w_ref):
    @pl.when(pl.program_id(0) == 0)
    def _():
        fill_weight(order_ref, pack_ref, 0, 3 * width // 128, w_ref, width // PARTS, width // 128)
        sums_ref[...] = jnp.zeros_like(sums_ref)

    back = dot_nt(grads_ref[0], w_ref[0]) + dot_nt(grads_ref[1], w_ref[1]) + dot_nt(grads_ref[2], w_ref[2])
    part, gain_sum = norm_back(x_ref[...].astype(F32), back, gain_ref[...])
    out_ref[...] = (middle_ref[...] + part).astype(BF)
    sums_ref[0:1, :] += gain_sum
    sums_ref[1:2, :] += jnp.sum(back, axis=0, keepdims=True)


def input_grad(order, pack, x, grads, middle_grad, gain):
    rows, width = x.shape
    block = min(256, rows)
    by_rows = pl.BlockSpec((block, width), lambda i, *_: (i, 0))
    return pl.pallas_call(
        functools.partial(input_kernel, width),
        grid_spec=pltpu.PrefetchScalarGridSpec(
            num_scalar_prefetch=1,
            grid=(rows // block,),
            in_specs=[
                whole_spec(pack.shape),
                by_rows,
                pl.BlockSpec((3, block, width), lambda i, *_: (0, i, 0)),
                by_rows,
                whole_spec(gain.shape),
            ],
            out_specs=[by_rows, whole_spec((8, width))],
            scratch_shapes=[pltpu.VMEM((3, width, width), BF)],
        ),
        out_shape=[
            jax.ShapeDtypeStruct((rows, width), BF),
            jax.ShapeDtypeStruct((8, width), F32),
        ],
        compiler_params=params(40),
        cost_estimate=cost(6 * rows * width * width, 18 * rows * width),
        name="input_grad",
    )(order, pack, x, grads, middle_grad, gain)


def tiles(matrix):
    rows, cols = matrix.shape
    return matrix.reshape(rows, cols // 128, 128).transpose(1, 0, 2).reshape(-1, 128)


def untiles(packed, rows):
    return packed.reshape(-1, rows, 128).transpose(1, 0, 2).reshape(rows, -1)


def scatter(part):
    return lax.psum(lax.psum_scatter(part, "shard", scatter_dimension=0, tiled=True), "rep")


def pack_weights(triple, output, expand, reduce, vectors):
    share, width = output.shape
    flat = jnp.concatenate(vectors)
    flat = jnp.pad(flat, (0, 2048 - flat.shape[0])).reshape(16, 128)
    up = expand.reshape(share, PARTS, CHUNKS, 128)
    down = reduce.reshape(CHUNKS, 128, width)
    return (
        jnp.concatenate([tiles(triple), flat]),
        tiles(output),
        *[jnp.concatenate([tiles(up[:, :, at].reshape(share, -1)), tiles(down[at])]) for at in range(CHUNKS)],
    )


def unpack_grads(share, grad_a, grad_b, *grads_c):
    half = PARTS * share
    ups = [untiles(one[:half], share).reshape(share, PARTS, 1, 128) for one in grads_c]
    downs = [untiles(one[half:], 128) for one in grads_c]
    return (
        untiles(grad_a, share),
        untiles(grad_b, share),
        jnp.concatenate(ups, axis=2).reshape(share, -1),
        jnp.concatenate(downs, axis=0),
    )


def shards(
    count,
    tokens,
    segments,
    cotangent,
    attend_gain,
    attend_shift,
    triple_weight,
    triple_bias,
    output_weight,
    output_bias,
    feed_gain,
    feed_shift,
    expand_weight,
    expand_bias,
    reduce_weight,
    reduce_bias,
):
    rows, width = tokens.shape
    small = (
        attend_gain, attend_shift, triple_bias, output_bias, feed_gain, feed_shift, expand_bias, reduce_bias
    )
    order = jnp.zeros((1,), jnp.int32)
    share = width // PARTS
    weights = (triple_weight, output_weight, expand_weight, reduce_weight, small)
    if count == PARTS:
        packs = [
            lax.all_gather(one, "shard", axis=0, tiled=True).reshape(PARTS, -1, 128) for one in pack_weights(*weights)
        ]
    else:
        weights = jax.tree.map(lambda one: lax.all_gather(one, "shard", axis=0, tiled=True), weights)
        weights = jax.tree.map(lambda one: one.reshape(PARTS, -1, *one.shape[1:]), weights)
        packs = jax.vmap(pack_weights)(*weights)
    pack_a, pack_b, *pack_c = packs
    vectors = pack_a[:, -16:, :].reshape(PARTS, 2048).astype(F32)
    whole, at = [], 0
    for one in small:
        size = one.shape[0] * count // PARTS
        whole.append(vectors[:, at : at + size].reshape(1, -1))
        at += size
    gain_one, shift_one, bias_qv, bias_out, gain_two, shift_two, bias_up, bias_down = whole
    bias_qkv = jnp.concatenate([bias_qv[:, :width], jnp.zeros((1, width), F32), bias_qv[:, width:]], axis=1)
    bias_qkv = bias_qkv.reshape(3, 1, width)
    bias_up = bias_up.reshape(PARTS, CHUNKS, 128)
    col = segments.reshape(rows, 1)
    row = segments.reshape(1, rows)

    qkv, turned_one = project(order, pack_a, tokens, gain_one, shift_one, bias_qkv)
    mixed, log_total = attend_forward(col, row, qkv)
    middle, normed_two, turned_two, feed = make_middle(
        order, pack_b, tokens, mixed, col, cotangent, bias_out, gain_two, shift_two
    )
    sums = ()
    grads_c, sums_c = [], []
    for at in range(CHUNKS):
        out_sum, back_sum, grad_c, sum_c = feed_chunk(
            order, pack_c[at], normed_two, turned_two, feed, bias_up[:, at].reshape(1, -1), sums
        )
        sums = (out_sum, back_sum)
        grads_c.append(grad_c)
        sums_c.append(sum_c.reshape(PARTS, 128))
    out_tokens, middle_grad, mixed_grad, grad_b, sums_two = branch(
        order, pack_b, back_sum, middle, out_sum, feed, col, mixed, gain_two, bias_down
    )
    projected_grad = attend_backward(col, row, qkv, mixed, log_total, mixed_grad)
    grad_a, sums_qkv = triple_grad(order, turned_one, projected_grad)
    grad_tokens, sums_one = input_grad(order, pack_a, tokens, projected_grad, middle_grad, gain_one)

    vectors = jnp.concatenate(
        [
            sums_one[0].reshape(PARTS, -1),
            sums_one[1].reshape(PARTS, -1),
            jnp.concatenate([sums_qkv[:, :width], sums_qkv[:, 2 * width :]], axis=1).reshape(PARTS, -1),
            sums_two[2].reshape(PARTS, -1),
            sums_two[0].reshape(PARTS, -1),
            sums_two[1].reshape(PARTS, -1),
            sums_c[0],
            sums_c[1],
            sums_c[2],
            sums_two[3].reshape(PARTS, -1),
        ],
        axis=1,
    )
    vectors = vectors.astype(BF)
    grads = (grad_a, grad_b, *grads_c)
    if count == PARTS:
        grads = [scatter(one.reshape(-1, 128)) for one in grads]
        grads = unpack_grads(share, *grads)
        vectors = jnp.pad(vectors, ((0, 0), (0, 2048 - vectors.shape[1]))).reshape(-1, 128)
        vectors = scatter(vectors).reshape(-1)
        small_grads, at = [], 0
        for one in small:
            small_grads.append(vectors[at : at + one.shape[0]])
            at += one.shape[0]
    else:
        grads = jax.vmap(functools.partial(unpack_grads, share))(*grads)
        grads = [scatter(one.reshape(-1, one.shape[-1])) for one in grads]
        small_grads, at = [], 0
        for one in small:
            size = one.shape[0] * count // PARTS
            small_grads.append(scatter(vectors[:, at : at + size].reshape(-1)))
            at += size
    grads = [one.astype(F32) for one in grads]
    small_grads = [one.astype(F32) for one in small_grads]
    return (
        out_tokens,
        grad_tokens,
        small_grads[0],
        small_grads[1],
        grads[0],
        small_grads[2],
        grads[1],
        small_grads[3],
        small_grads[4],
        small_grads[5],
        grads[2],
        small_grads[6],
        grads[3],
        small_grads[7],
    )


def solution(mesh):
    return jax.shard_map(
        functools.partial(shards, mesh.shape["shard"]),
        mesh=mesh,
        in_specs=(
            P(("shard", "rep"), None),
            P(("shard", "rep")),
            P(("shard", "rep"), None),
            P("shard"),
            P("shard"),
            P("shard", None),
            P("shard"),
            P("shard", None),
            P("shard"),
            P("shard"),
            P("shard"),
            P("shard", None),
            P("shard"),
            P("shard", None),
            P("shard"),
        ),
        out_specs=(
            P(("shard", "rep"), None),
            P(("shard", "rep"), None),
            P("shard"),
            P("shard"),
            P("shard", None),
            P("shard"),
            P("shard", None),
            P("shard"),
            P("shard"),
            P("shard"),
            P("shard", None),
            P("shard"),
            P("shard", None),
            P("shard"),
        ),
        check_vma=False,
    )
```

```python
import functools

import jax
import jax.numpy as jnp
from jax import lax
from jax.experimental import pallas as pl
from jax.experimental.pallas import tpu as pltpu
from jax.sharding import PartitionSpec as P

HEAD_DIM = 64
PARTS = 8
HALVES = 3
GAIN_ONE, SHIFT_ONE, BIAS_OUT, GAIN_TWO, SHIFT_TWO, BIAS_DOWN, BIAS_QV = range(7)
VECTOR_ROWS = ((0,), (1,), (2,), (3,), (4,), (5,), (6, 7))
EPSILON = 1e-05
BF = jnp.bfloat16
F32 = jnp.float32
NEVER = -1e30
ROOT = 0.7978845608028654
MIB = 1 << 20
VMEM = 60


def dot_nn(left, right):
    return lax.dot_general(left, right, (((1,), (0,)), ((), ())), preferred_element_type=F32)


def dot_nt(left, right):
    return lax.dot_general(left, right, (((1,), (1,)), ((), ())), preferred_element_type=F32)


def dot_tn(left, right):
    return lax.dot_general(left, right, (((0,), (0,)), ((), ())), preferred_element_type=F32)


def normalise(values):
    center = values - jnp.mean(values, axis=-1, keepdims=True)
    variance = jnp.mean(center * center, axis=-1, keepdims=True)
    scale = lax.rsqrt(variance + EPSILON)
    return center * scale, scale


def norm_back(values, incoming, gain):
    unit, scale = normalise(values)
    scaled = incoming * gain
    first = jnp.mean(scaled, axis=-1, keepdims=True)
    second = jnp.mean(scaled * unit, axis=-1, keepdims=True)
    back = scale * (scaled - first - unit * second)
    return back, jnp.sum(incoming * unit, axis=0, keepdims=True)


def whole_spec(shape):
    return pl.BlockSpec(shape, lambda *_: (0,) * len(shape))


def once_spec(shape):
    return pl.BlockSpec(shape, lambda *_: (0,) * len(shape), pipeline_mode=pl.Buffered(1))


def cost(flops, moved, exps=0):
    return pl.CostEstimate(flops=int(flops), bytes_accessed=int(moved), transcendentals=int(exps))


def run(kernel, name, order, deps, inputs, in_specs, out_specs, out_shape, scratch=(), grid=(1,), estimate=None):
    count = len(deps)

    def body(order_ref, *refs):
        kernel(order_ref, *refs[count:])

    return pl.pallas_call(
        body,
        grid_spec=pltpu.PrefetchScalarGridSpec(
            num_scalar_prefetch=1,
            grid=grid,
            in_specs=[pl.BlockSpec(memory_space=pl.ANY)] * count + list(in_specs),
            out_specs=out_specs,
            scratch_shapes=list(scratch),
        ),
        out_shape=out_shape,
        compiler_params=pltpu.CompilerParams(vmem_limit_bytes=VMEM * MIB),
        cost_estimate=estimate,
        name=name,
    )(order, *deps, *inputs)


def gate(deps, *values):
    count, size = len(deps), len(values)
    return pl.pallas_call(
        lambda *_: None,
        in_specs=[pl.BlockSpec(memory_space=pl.ANY)] * (count + size),
        out_specs=[pl.BlockSpec(memory_space=pl.ANY)] * size,
        out_shape=[jax.ShapeDtypeStruct(one.shape, one.dtype) for one in values],
        input_output_aliases={count + at: at for at in range(size)},
        name="gate",
    )(*deps, *values)


def fill_weight(order_ref, pieces, first, blocks, out_ref, rows, lead=None):
    mine = order_ref[0]
    for piece in range(PARTS):
        place = pl.ds(pl.multiple_of((piece ^ mine) * rows, 32), rows)
        for at in range(blocks):
            tile = piece_rows(pieces, piece, first + at * rows, rows)
            if lead is None:
                out_ref[place, at * 128 : (at + 1) * 128] = tile
            else:
                group, inside = divmod(at, lead)
                out_ref[group, place, inside * 128 : (inside + 1) * 128] = tile


def piece_rows(pieces, piece, start, rows):
    if len(pieces) == PARTS or piece < 6:
        return pieces[piece][start : start + rows, :]
    cut = pieces[6].shape[0]
    if start < cut:
        return pieces[2 * piece - 6][start : start + rows, :]
    return pieces[2 * piece - 5][start - cut : start - cut + rows, :]


def put_pieces(order_ref, even_ref, odd_ref, place, value):
    chip = lax.shift_right_logical(order_ref[0], 1)
    for core in range(2):
        @pl.when(lax.rem(order_ref[0], 2) == core)
        def _():
            for part in range(PARTS):
                out_ref = even_ref if part % 2 == core else odd_ref
                out_ref[(part // 2) ^ chip, place, :] = value(part)


def project_kernel(width, count, order_ref, *refs):
    pieces, (x_ref, qkv_ref, turned_ref, vector_ref, up_ref, w_ref, v_ref) = refs[:count], refs[count:]
    share = width // PARTS

    @pl.when(pl.program_id(0) == 0)
    def _():
        fill_weight(order_ref, pieces, 0, 3 * width // 128, w_ref, share, width // 128)
        for piece in range(PARTS):
            v_ref[piece ^ order_ref[0]] = piece_rows(pieces, piece, 3 * width // 128 * share, 16).astype(F32)
        vector_ref[...] = jnp.zeros_like(vector_ref)
        for out, places in enumerate(VECTOR_ROWS):
            parts = [
                v_ref[at // len(places), places[at % len(places)] : places[at % len(places)] + 1, :share]
                for at in range(PARTS * len(places))
            ]
            for at in range(len(places)):
                row = jnp.concatenate(parts[at * PARTS : (at + 1) * PARTS], axis=1)
                vector_ref[out + at : out + at + 1, :] = row
        wide = up_ref.shape[1] // PARTS // 128
        for part in range(PARTS):
            for at in range(wide):
                first = (part * wide + at) * 128
                up_ref[:, first : first + 128] = v_ref[part, 8 + at : 9 + at, :]

    unit, _ = normalise(x_ref[...].astype(F32))
    normed = (unit * vector_ref[GAIN_ONE : GAIN_ONE + 1, :] + vector_ref[SHIFT_ONE : SHIFT_ONE + 1, :]).astype(BF)
    turned_ref[...] = normed.T
    for at in range(3):
        product = dot_nn(normed, w_ref[at])
        if at != 1:
            product = product + vector_ref[BIAS_QV + at // 2 : BIAS_QV + at // 2 + 1, :]
        qkv_ref[at] = product.astype(BF)


def project(order, deps, pack, x, hidden):
    rows, width = x.shape
    block = min(256, rows)
    return run(
        functools.partial(project_kernel, width, len(pack)),
        "project",
        order,
        deps,
        (*pack, x),
        [whole_spec(one.shape) for one in pack] + [pl.BlockSpec((block, width), lambda i, *_: (i, 0))],
        [
            pl.BlockSpec((3, block, width), lambda i, *_: (0, i, 0)),
            pl.BlockSpec((width, block), lambda i, *_: (0, i)),
            whole_spec((8, width)),
            whole_spec((1, hidden)),
        ],
        [
            jax.ShapeDtypeStruct((3, rows, width), BF),
            jax.ShapeDtypeStruct((width, rows), BF),
            jax.ShapeDtypeStruct((8, width), F32),
            jax.ShapeDtypeStruct((1, hidden), F32),
        ],
        [pltpu.VMEM((3, width, width), BF), pltpu.VMEM((PARTS, 16, 128), F32)],
        (rows // block,),
        cost(6 * rows * width * width, 14 * rows * width),
    )


def attend_forward_kernel(block, order_ref, col_ref, row_ref, qkv_ref, mixed_ref, log_ref, bias_ref):
    rows = row_ref.shape[1]

    @pl.when(pl.program_id(0) == 0)
    def _():
        for first in range(0, rows, block):
            at = lax.broadcasted_iota(jnp.int32, (block, rows), 0) + first
            key = lax.broadcasted_iota(jnp.int32, (block, rows), 1)
            same = col_ref[first : first + block, :] == row_ref[...]
            bias_ref[first : first + block, :] = jnp.where(same & (key <= at), 0.0, NEVER)

    lane = lax.broadcasted_iota(jnp.int32, (block, 128), 1)
    for first in range(0, rows, block):
        last = first + block
        queries = qkv_ref[0, first:last, :] * jnp.asarray(0.125, BF)
        outs, logs = [], []
        for head in range(2):
            mine = (lane < HEAD_DIM) if head == 0 else (lane >= HEAD_DIM)
            scores = dot_nt(jnp.where(mine, queries, jnp.zeros_like(queries)), qkv_ref[1, :last, :])
            scores = scores + bias_ref[first:last, :last]
            largest = jnp.max(scores, axis=-1, keepdims=True)
            expo = jnp.exp(scores - largest)
            total = jnp.sum(expo, axis=-1, keepdims=True)
            outs.append(dot_nn(expo.astype(BF), qkv_ref[2, :last, :]) / total)
            logs.append(largest + jnp.log(total))
        mixed_ref[first:last, :] = jnp.where(lane < HEAD_DIM, outs[0], outs[1]).astype(BF)
        log_ref[0, first:last, :] = jnp.where(lane < HEAD_DIM, logs[1], logs[0])


def attend_forward(order, deps, col, row, qkv, half):
    _, rows, width = qkv.shape
    pairs = width // 128 // HALVES
    block = min(256, rows)
    return run(
        functools.partial(attend_forward_kernel, block),
        "attend_forward",
        order,
        deps,
        (col, row, qkv),
        [
            whole_spec(col.shape),
            whole_spec(row.shape),
            pl.BlockSpec((3, rows, 128), lambda i, *_: (0, 0, i + half * pairs)),
        ],
        [
            pl.BlockSpec((rows, 128), lambda i, *_: (0, i)),
            pl.BlockSpec((1, rows, 128), lambda i, *_: (i, 0, 0)),
        ],
        [
            jax.ShapeDtypeStruct((rows, width // HALVES), BF),
            jax.ShapeDtypeStruct((pairs, rows, 128), F32),
        ],
        [pltpu.VMEM((rows, rows), F32)],
        (pairs,),
        cost(8 * rows * rows * width, 6 * rows * width, rows * rows * pairs),
    )


def split_lanes(value, lane):
    high = value.astype(BF)
    rest = value - high.astype(F32)
    middle = rest.astype(BF)
    low = (rest - middle.astype(F32)).astype(BF)
    inside = lax.rem(lane, HEAD_DIM)
    zero = jnp.zeros_like(high)
    return jnp.where(inside == 0, high, jnp.where(inside == 1, middle, jnp.where(inside == 2, low, zero)))


def attend_backward_kernel(
    block, order_ref, col_ref, row_ref, qkv_ref, mixed_ref, log_ref, grad_ref, out_ref, bias_ref, q_ref, k_ref, d_ref, v_ref,
    dq_ref,
):
    rows = row_ref.shape[1]

    @pl.when(pl.program_id(0) == 0)
    def _():
        for first in range(0, rows, block):
            key = lax.broadcasted_iota(jnp.int32, (block, rows), 0) + first
            at = lax.broadcasted_iota(jnp.int32, (block, rows), 1)
            same = col_ref[first : first + block, :] == row_ref[...]
            bias_ref[first : first + block, :] = jnp.where(same & (key <= at), 0.0, NEVER)

    lane = lax.broadcasted_iota(jnp.int32, (block, 128), 1)
    below = lane < HEAD_DIM
    minus = jnp.where(lax.rem(lane, HEAD_DIM) < 3, -1.0, 0.0).astype(BF)
    for first in range(0, rows, block):
        last = first + block
        queries = qkv_ref[0, first:last, :] * jnp.asarray(0.125, BF)
        keys = qkv_ref[1, first:last, :]
        values = qkv_ref[2, first:last, :]
        grads = grad_ref[first:last, :]
        product = grads.astype(F32) * mixed_ref[first:last, :].astype(F32)
        sums = [
            jnp.sum(jnp.where(below, product, 0.0), axis=-1, keepdims=True),
            jnp.sum(jnp.where(below, 0.0, product), axis=-1, keepdims=True),
        ]
        logs = split_lanes(log_ref[0, first:last, :], lane)
        inner = split_lanes(jnp.where(below, sums[1], sums[0]), lane)
        for head in range(2):
            mine = below if head == 0 else lane >= HEAD_DIM
            q_ref[head, first:last, :] = jnp.where(mine, queries, logs)
            k_ref[head, first:last, :] = jnp.where(mine, keys, minus)
            d_ref[head, first:last, :] = jnp.where(mine, grads, inner)
            v_ref[head, first:last, :] = jnp.where(mine, values, minus)

    for first in range(0, rows, block):
        last = first + block
        key_parts, value_parts, query_parts = [], [], []
        for head in range(2):
            scores = dot_nt(k_ref[head, first:last, :], q_ref[head, first:, :]) + bias_ref[first:last, first:]
            probs = jnp.exp(scores)
            slopes = probs * dot_nt(v_ref[head, first:last, :], d_ref[head, first:, :])
            slopes = slopes.astype(BF)
            value_parts.append(dot_nn(probs.astype(BF), d_ref[head, first:, :]))
            key_parts.append(dot_nn(slopes, q_ref[head, first:, :]))
            query_parts.append(dot_tn(slopes, k_ref[head, first:last, :]))
        out_ref[1, first:last, :] = jnp.where(below, key_parts[0], key_parts[1]).astype(BF)
        out_ref[2, first:last, :] = jnp.where(below, value_parts[0], value_parts[1]).astype(BF)
        side = lax.broadcasted_iota(jnp.int32, (rows - first, 128), 1) < HEAD_DIM
        part = jnp.where(side, query_parts[0], query_parts[1])
        if first == 0:
            dq_ref[...] = part
        else:
            dq_ref[first:, :] += part
    out_ref[0] = (dq_ref[...] * 0.125).astype(BF)


def attend_backward(order, deps, col, row, qkv, mixed, log_total, grad, half):
    _, rows, width = qkv.shape
    pairs = width // 128 // HALVES
    block = min(256, rows)
    return run(
        functools.partial(attend_backward_kernel, block),
        "attend_backward",
        order,
        deps,
        (col, row, qkv, mixed, log_total, grad),
        [
            whole_spec(col.shape),
            whole_spec(row.shape),
            pl.BlockSpec((3, rows, 128), lambda i, *_: (0, 0, i + half * pairs)),
            pl.BlockSpec((rows, 128), lambda i, *_: (0, i)),
            pl.BlockSpec((1, rows, 128), lambda i, *_: (i, 0, 0)),
            pl.BlockSpec((rows, 128), lambda i, *_: (0, i + half * pairs)),
        ],
        pl.BlockSpec((3, rows, 128), lambda i, *_: (0, 0, i)),
        jax.ShapeDtypeStruct((3, rows, width // HALVES), BF),
        [pltpu.VMEM((rows, rows), F32)] + [pltpu.VMEM((2, rows, 128), BF)] * 4 + [pltpu.VMEM((rows, 128), F32)],
        (pairs,),
        cost(20 * rows * rows * width, 10 * rows * width, rows * rows * pairs),
    )


def middle_kernel(width, hidden, steps, count, order_ref, *refs):
    pieces, refs = refs[:count], refs[count:]
    x_ref, seg_ref, cot_ref, vector_ref, bias_ref, *refs = refs
    mixed_refs, refs = refs[:HALVES], refs[HALVES:]
    turned_ref, feed_ref, h_ref, e_ref, out_ref, grad_ref, branch_ref, mixed_grad_ref, sums_ref, wide_ref, *refs = refs
    wo_ref, we_ref, wr_ref = refs
    share = width // PARTS

    @pl.when(pl.program_id(0) == 0)
    def _():
        fill_weight(order_ref, pieces, 0, width // 128, wo_ref, share)
        fill_weight(order_ref, pieces, width // 128 * share, hidden // 128, we_ref, share)
        fill_weight(order_ref, pieces, (width + hidden) // 128 * share, width // 128, wr_ref, hidden // PARTS)
        sums_ref[...] = jnp.zeros_like(sums_ref)
        wide_ref[...] = jnp.zeros_like(wide_ref)

    def vector(at):
        return vector_ref[at : at + 1, :]

    mixed = jnp.concatenate([one[...] for one in mixed_refs], axis=1)
    middle = x_ref[...].astype(F32) + dot_nn(mixed, wo_ref[...]) + vector(BIAS_OUT)
    unit, scale = normalise(middle)
    normed = (unit * vector(GAIN_TWO) + vector(SHIFT_TWO)).astype(BF)
    turned_ref[...] = normed.T
    live = seg_ref[...] >= 0
    feed = jnp.where(live, cot_ref[...].astype(F32), 0.0)
    feed_low = feed.astype(BF)
    feed_ref[...] = feed_low
    for at in range(0, hidden, 256):
        cols = slice(at, at + 256)
        u = dot_nn(normed, we_ref[:, cols]) + bias_ref[:, cols]
        hidden_grad = dot_nt(feed_low, wr_ref[cols, :])
        square = u * u
        tanh = jnp.tanh(u * (ROOT + (ROOT * 0.044715) * square))
        half = 0.5 + 0.5 * tanh
        h_ref[:, cols] = (u * half).astype(BF)
        slope = half + u * (0.5 - 0.5 * (tanh * tanh)) * (ROOT + (3 * 0.044715 * ROOT) * square)
        e_part = (hidden_grad * slope).astype(BF)
        e_ref[:, cols] = e_part
        wide_ref[:, cols] += jnp.sum(e_part.astype(F32), axis=0, keepdims=True)
    total = middle + dot_nn(h_ref[...], wr_ref[...]) + vector(BIAS_DOWN)
    out_ref[...] = jnp.where(live, total, 0.0).astype(BF)
    back = dot_nt(e_ref[...], we_ref[...])
    scaled = back * vector(GAIN_TWO)
    mean = jnp.mean(scaled, axis=-1, keepdims=True)
    second = jnp.mean(scaled * unit, axis=-1, keepdims=True)
    grad = feed + scale * (scaled - mean - unit * second)
    grad_ref[...] = grad
    branch = grad.astype(BF)
    branch_ref[...] = branch
    mixed_grad_ref[...] = dot_nt(branch, wo_ref[...]).astype(BF)
    sums_ref[0:1, :] += jnp.sum(back * unit, axis=0, keepdims=True)
    sums_ref[1:2, :] += jnp.sum(back, axis=0, keepdims=True)
    sums_ref[2:3, :] += jnp.sum(branch.astype(F32), axis=0, keepdims=True)
    sums_ref[3:4, :] += jnp.sum(feed, axis=0, keepdims=True)


def make_middle(order, deps, pack, x, mixed, col, cot, vectors, bias):
    rows, width = x.shape
    hidden = bias.shape[1]
    block = min(256, rows)
    by_rows = pl.BlockSpec((block, width), lambda i, *_: (i, 0))
    by_wide = pl.BlockSpec((block, hidden), lambda i, *_: (i, 0))
    low = jax.ShapeDtypeStruct((rows, width), BF)
    return run(
        functools.partial(middle_kernel, width, hidden, rows // block, len(pack)),
        "middle",
        order,
        deps,
        (*pack, x, col, cot, vectors, bias, *mixed),
        [once_spec(one.shape) for one in pack]
        + [by_rows, pl.BlockSpec((block, 1), lambda i, *_: (i, 0)), by_rows]
        + [whole_spec(vectors.shape), whole_spec(bias.shape)]
        + [pl.BlockSpec((block, width // HALVES), lambda i, *_: (i, 0))] * HALVES,
        [pl.BlockSpec((width, block), lambda i, *_: (0, i)), by_rows, by_wide, by_wide]
        + [by_rows] * 4
        + [whole_spec((8, width)), whole_spec((1, hidden))],
        [
            jax.ShapeDtypeStruct((width, rows), BF),
            low,
            jax.ShapeDtypeStruct((rows, hidden), BF),
            jax.ShapeDtypeStruct((rows, hidden), BF),
            low,
            jax.ShapeDtypeStruct((rows, width), F32),
            low,
            low,
            jax.ShapeDtypeStruct((8, width), F32),
            jax.ShapeDtypeStruct((1, hidden), F32),
        ],
        [pltpu.VMEM((width, width), BF), pltpu.VMEM((width, hidden), BF), pltpu.VMEM((hidden, width), BF)],
        (rows // block,),
        cost(4 * rows * width * (width + 2 * hidden), 50 * rows * width, rows * hidden),
    )


def down_kernel(order_ref, h_ref, feed_ref, even_ref, odd_ref):
    grad = dot_tn(h_ref[...], feed_ref[...]).astype(BF)
    half, width = grad.shape[0] // 2, grad.shape[1]
    for core in range(2):
        @pl.when(lax.rem(order_ref[0], 2) == core)
        def _():
            for side in range(2):
                out_ref = even_ref if side == core else odd_ref
                for lane in range(width // 128):
                    out_ref[0, lane * half : (lane + 1) * half, :] = grad[
                        side * half : (side + 1) * half, lane * 128 : (lane + 1) * 128
                    ]


def down_grad(order, deps, h, feed):
    rows, hidden = h.shape
    width = feed.shape[1]
    pairs = PARTS // 2
    own = jax.ShapeDtypeStruct((pairs, hidden // PARTS * width // 128, 128), BF)
    own_spec = pl.BlockSpec((1, *own.shape[1:]), lambda i, order: (i ^ lax.shift_right_logical(order[0], 1), 0, 0))
    return run(
        down_kernel,
        "down_grad",
        order,
        deps,
        (h, feed),
        [pl.BlockSpec((rows, hidden // pairs), lambda i, *_: (0, i)), whole_spec(feed.shape)],
        [own_spec, own_spec],
        [own, own],
        (),
        (pairs,),
        cost(2 * rows * width * hidden, 4 * rows * hidden),
    )


def up_kernel(steps, order_ref, *refs):
    turned_ref, e_ref, branch_ref, sums_ref, wide_ref, *refs = refs
    mixed_refs, (even_ref, odd_ref, own_even_ref, own_odd_ref, t_ref) = refs[:HALVES], refs[HALVES:]
    step = pl.program_id(0)

    @pl.when(step < steps)
    def _():
        put_triple(order_ref, turned_ref[...], e_ref[...], even_ref, odd_ref, 0, False)

    @pl.when(step == steps)
    def _():
        width = branch_ref.shape[1]
        share, half = width // PARTS, width // 256
        third = width // HALVES
        for at, one in enumerate(mixed_refs):
            t_ref[at * third : (at + 1) * third, :] = dot_tn(one[...], branch_ref[...]).astype(BF)
        for lane in range(width // 128):
            base = lane * share + lane // half * 16
            put_pieces(
                order_ref, own_even_ref, own_odd_ref, slice(base, base + share),
                lambda part: t_ref[part * share : (part + 1) * share, lane * 128 : (lane + 1) * 128],
            )
        put_vectors(
            order_ref, own_even_ref, own_odd_ref, half * share, sums_ref,
            lambda part: [(at, part) for at in range(4)], wide_ref,
        )
        for one in (own_even_ref, own_odd_ref):
            one[:, 2 * half * share + 16 :, :] = jnp.zeros((PARTS // 2, 16, 128), BF)


def up_grad(order, deps, turned, e, branch, sums, wide, mixed):
    width, rows = turned.shape
    hidden = e.shape[1]
    steps = PARTS // 2
    share = width // PARTS
    part_rows = hidden // steps // 128 * share
    up = jax.ShapeDtypeStruct((PARTS // 2, hidden // 128 * share, 128), BF)
    own = jax.ShapeDtypeStruct((PARTS // 2, width // 128 * share + 32, 128), BF)
    up_spec = pl.BlockSpec((PARTS // 2, part_rows, 128), lambda i, *_: (0, jnp.minimum(i, steps - 1), 0))
    return run(
        functools.partial(up_kernel, steps),
        "up_grad",
        order,
        deps,
        (turned, e, branch, sums, wide, *mixed),
        [whole_spec(turned.shape), pl.BlockSpec((rows, hidden // steps), lambda i, *_: (0, jnp.minimum(i, steps - 1)))]
        + [whole_spec(one.shape) for one in (branch, sums, wide, *mixed)],
        [up_spec, up_spec, whole_spec(own.shape), whole_spec(own.shape)],
        [up, up, own, own],
        [pltpu.VMEM((width, width), BF)],
        (steps + 1,),
        cost(2 * rows * width * (hidden + width), 4 * rows * hidden),
    )


def put_vectors(order_ref, even_ref, odd_ref, base, sums_ref, shares, wide_ref=None):
    share = sums_ref.shape[1] // PARTS
    sums = sums_ref[...]
    blank = jnp.zeros((1, 128 - share), F32)

    def value(part):
        rows = [
            jnp.concatenate([sums[row : row + 1, at * share : (at + 1) * share], blank], axis=1)
            for row, at in shares(part)
        ]
        if wide_ref is not None:
            size = wide_ref.shape[1] // PARTS
            rows += [wide_ref[:, at : at + 128] for at in range(part * size, (part + 1) * size, 128)]
        rows.append(jnp.zeros((16 - len(rows), 128), F32))
        return jnp.concatenate(rows, axis=0).astype(BF)

    put_pieces(order_ref, even_ref, odd_ref, slice(base, base + 16), value)


def put_triple(order_ref, turned, grads, even_ref, odd_ref, base, summed=True):
    share = turned.shape[0] // PARTS
    product = dot_nn(turned, grads).astype(BF)
    for lane in range(grads.shape[1] // 128):
        put_pieces(
            order_ref, even_ref, odd_ref, pl.ds(base + lane * share, share),
            lambda part: product[part * share : (part + 1) * share, lane * 128 : (lane + 1) * 128],
        )
    return jnp.sum(grads.astype(F32), axis=0, keepdims=True) if summed else None


def triple_kernel(order_ref, turned_ref, first_ref, second_ref, even_ref, odd_ref, sum_ref):
    part_rows = even_ref.shape[1] // 2
    third = first_ref.shape[2]
    sum_ref[0, :, :third] = put_triple(order_ref, turned_ref[...], first_ref[0], even_ref, odd_ref, 0)
    sum_ref[0, :, third:] = put_triple(order_ref, turned_ref[...], second_ref[0], even_ref, odd_ref, part_rows)


def triple_grad(order, deps, turned, first, second):
    width, rows = turned.shape
    third = first.shape[2]
    part_rows = 2 * third // 128 * width // PARTS
    own = jax.ShapeDtypeStruct((PARTS // 2, 3 * part_rows, 128), BF)
    own_spec = pl.BlockSpec((PARTS // 2, part_rows, 128), lambda i, *_: (0, i, 0))
    by_third = pl.BlockSpec((1, rows, third), lambda i, *_: (i, 0, 0))
    return run(
        triple_kernel,
        "triple_grad",
        order,
        deps,
        (turned, first, second),
        [whole_spec(turned.shape), by_third, by_third],
        [own_spec, own_spec, pl.BlockSpec((1, 1, 2 * third), lambda i, *_: (i, 0, 0))],
        [own, own, jax.ShapeDtypeStruct((3, 1, 2 * third), F32)],
        (),
        (3,),
        cost(12 * rows * width * third, 8 * rows * width),
    )


def last_kernel(width, steps, count, order_ref, *refs):
    pieces, refs = refs[:count], refs[count:]
    x_ref, turned_ref, *refs = refs
    third_refs, refs = refs[:HALVES], refs[HALVES:]
    whole_ref, middle_ref, vector_ref, sum_ref, even_ref, odd_ref, out_ref, w_ref, sums_ref, late_ref = refs
    step = pl.program_id(0)
    share, third = width // PARTS, width // HALVES
    part_rows = third // 128 * share

    @pl.when(step == 0)
    def _():
        fill_weight(order_ref, pieces, 0, 3 * width // 128, w_ref, share, width // 128)
        sums_ref[...] = jnp.zeros_like(sums_ref)

    @pl.when(step < 3)
    def _():
        base = pl.multiple_of(step * part_rows, 32)
        late_ref[step] = put_triple(order_ref, turned_ref[...], whole_ref[0], even_ref, odd_ref, base)

    @pl.when(step >= 3)
    def _():
        back = None
        for at in range(3):
            one = dot_nt(jnp.concatenate([ref[at] for ref in third_refs], axis=1), w_ref[at])
            back = one if back is None else back + one
        part, gain_sum = norm_back(x_ref[...].astype(F32), back, vector_ref[GAIN_ONE : GAIN_ONE + 1, :])
        out_ref[...] = (middle_ref[...] + part).astype(BF)
        sums_ref[0:1, :] += gain_sum
        sums_ref[1:2, :] += jnp.sum(back, axis=0, keepdims=True)

    @pl.when(step == 3 + steps - 1)
    def _():
        for row, at in ((2, 0), (3, 2)):
            sums_ref[row : row + 1, : 2 * third] = sum_ref[at]
            sums_ref[row : row + 1, 2 * third :] = late_ref[at]
        put_vectors(
            order_ref, even_ref, odd_ref, 3 * part_rows, sums_ref,
            lambda part: [(0, part), (1, part)]
            + [(2 + at // PARTS, at % PARTS) for at in (2 * part, 2 * part + 1)],
        )


def last_grads(order, deps, pack, x, turned, grads, middle_grad, vectors, sums):
    rows, width = x.shape
    third = width // HALVES
    block = min(256, rows)
    steps = rows // block
    own = jax.ShapeDtypeStruct((PARTS // 2, 3 * third // 128 * width // PARTS + 16, 128), BF)
    by_rows = pl.BlockSpec((block, width), lambda i, *_: (jnp.maximum(i - 3, 0), 0))
    by_third = pl.BlockSpec((3, block, third), lambda i, *_: (0, jnp.maximum(i - 3, 0), 0))
    return run(
        functools.partial(last_kernel, width, steps, len(pack)),
        "last_grads",
        order,
        deps,
        (*pack, x, turned, *grads, grads[-1], middle_grad, vectors, sums),
        [once_spec(one.shape) for one in pack]
        + [by_rows, whole_spec(turned.shape)]
        + [by_third] * HALVES
        + [
            pl.BlockSpec((1, rows, third), lambda i, *_: (jnp.minimum(i, 2), 0, 0)),
            by_rows,
            whole_spec(vectors.shape),
            whole_spec(sums.shape),
        ],
        [whole_spec(own.shape), whole_spec(own.shape), by_rows],
        [own, own, jax.ShapeDtypeStruct((rows, width), BF)],
        [pltpu.VMEM((3, width, width), BF), pltpu.VMEM((8, width), F32), pltpu.VMEM((3, 1, third), F32)],
        (3 + steps,),
        cost(8 * rows * width * width, 24 * rows * width),
    )


def owner_kernel(width, hidden, order_ref, mine_ref, other_ref, low_ref, low_other_ref, *outs):
    expand_ref, reduce_ref, output_ref, vector_ref = outs
    share, tall, half = width // PARTS, hidden // PARTS, width // 256
    ups = hidden // 256
    bit = order_ref[1] & 1
    for place in range(2):
        @pl.when(bit == place)
        def _():
            for side in range(2):
                up_ref, down_ref = (mine_ref, low_ref) if side == place else (other_ref, low_other_ref)
                for at in range(ups):
                    first = (side * ups + at) * 128
                    expand_ref[:, first : first + 128] = up_ref[at * share : (at + 1) * share, :].astype(F32)
                base = ups * share
                for at in range(half):
                    first = (side * half + at) * 128
                    output_ref[:, first : first + 128] = up_ref[
                        base + at * share : base + (at + 1) * share, :
                    ].astype(F32)
                    reduce_ref[:, first : first + 128] = down_ref[at * tall : (at + 1) * tall, :].astype(F32)
                if side == 0:
                    vector_ref[...] = up_ref[base + half * share : base + half * share + 16, :].astype(F32)


def owner_parts(order, deps, width, hidden, mine, other, low, low_other):
    share, tall = width // PARTS, hidden // PARTS
    shapes = [(share, hidden), (tall, width), (share, width), (16, 128)]
    return run(
        functools.partial(owner_kernel, width, hidden),
        "owner_parts",
        order,
        deps,
        (mine, other, low, low_other),
        [whole_spec(one.shape) for one in (mine, other, low, low_other)],
        [whole_spec(one) for one in shapes],
        [jax.ShapeDtypeStruct(one, F32) for one in shapes],
        (),
        (1,),
        cost(0, 6 * mine.size),
    )


def triple_owner_kernel(width, order_ref, *refs):
    first, last, (out_ref, vector_ref) = refs[:2], refs[2:4], refs[4:]
    share, tiles_each = width // PARTS, width // HALVES // 128
    for at in range(3):
        for third in range(HALVES):
            for tile in range(tiles_each):
                if third < 2:
                    start, terms = (2 * at + third) * tiles_each + tile, first
                else:
                    start, terms = at * tiles_each + tile, last
                rows = slice(start * share, (start + 1) * share)
                column = (at * HALVES + third) * tiles_each + tile
                total = terms[0][rows, :].astype(F32) + terms[1][rows, :].astype(F32)
                out_ref[:, column * 128 : (column + 1) * 128] = total
    rows = slice(3 * tiles_each * share, 3 * tiles_each * share + 16)
    vector_ref[...] = last[0][rows, :].astype(F32) + last[1][rows, :].astype(F32)


def triple_owner(order, deps, width, *terms):
    shapes = [(width // PARTS, 3 * width), (16, 128)]
    return run(
        functools.partial(triple_owner_kernel, width),
        "triple_owner",
        order,
        deps,
        terms,
        [whole_spec(one.shape) for one in terms],
        [whole_spec(one) for one in shapes],
        [jax.ShapeDtypeStruct(one, F32) for one in shapes],
        (),
        (1,),
        cost(0, 12 * terms[0].size),
    )


def tiles(matrix):
    rows, cols = matrix.shape
    return matrix.reshape(rows, cols // 128, 128).transpose(1, 0, 2).reshape(-1, 128)


def untiles(packed, rows):
    return packed.reshape(-1, rows, 128).transpose(1, 0, 2).reshape(rows, -1)


def swap(value, mask):
    return lax.ppermute(value, "shard", [(at, at ^ mask) for at in range(PARTS)])


def swap_rep(value, mask):
    count = lax.axis_size("rep")
    return lax.ppermute(value, "rep", [(at, at ^ mask) for at in range(count)])


def combine_kernel(plan, order_ref, *refs):
    outs = refs[len(refs) - len(plan) :]
    for out_ref, segments in zip(outs, plan):
        at = 0
        for rows, terms in segments:
            total = None
            for source, start in terms:
                ref = refs[source]
                if isinstance(start, tuple):
                    base, half, flip = start
                    bit = order_ref[1] & 1
                    start = pl.multiple_of(base + (1 - bit if flip else bit) * half, 16)
                    rows_at = pl.ds(start, rows)
                else:
                    rows_at = slice(start, start + rows)
                one = ref[0, rows_at, :] if len(ref.shape) == 3 else ref[rows_at, :]
                if len(terms) > 1:
                    one = one.astype(F32)
                total = one if total is None else total + one
            out_ref[at : at + rows, :] = total.astype(BF)
            at += rows


def combine(order, deps, *outs):
    arrays, specs, places, plan, shapes = [], [], {}, [], []
    for segments in outs:
        steps = []
        for rows, *terms in segments:
            sources = []
            for array, index, start in terms:
                key = (id(array), index)
                if key not in places:
                    places[key] = len(arrays)
                    arrays.append(array)
                    if index is None:
                        specs.append(whole_spec(array.shape))
                    else:
                        specs.append(pl.BlockSpec((1, *array.shape[1:]), lambda *_, index=index: (index, 0, 0)))
                sources.append((places[key], start))
            steps.append((rows, tuple(sources)))
        plan.append(tuple(steps))
        shapes.append(jax.ShapeDtypeStruct((sum(rows for rows, _ in steps), 128), BF))
    moved = sum(2 * 128 * one.shape[-2] for one in arrays) + sum(256 * one.shape[0] for one in shapes)
    return run(
        functools.partial(combine_kernel, tuple(plan)),
        "combine",
        order,
        deps,
        arrays,
        specs,
        [whole_spec(one.shape) for one in shapes],
        shapes,
        (),
        (1,),
        cost(0, moved),
    )


def pack_kernel(plan, order_ref, *refs):
    outs = refs[len(refs) - len(plan) :]
    for out_ref, blocks in zip(outs, plan):
        at = 0
        for source, first, rows, column, columns in blocks:
            if rows == 1 and columns:
                if at % 16 == 0:
                    out_ref[at : at + 16, :] = jnp.zeros((16, 128), BF)
            out_ref[at : at + rows, :columns] = refs[source][first : first + rows, column : column + columns]
            at += rows


def pack_parts(order, deps, inputs, plan):
    shapes = [jax.ShapeDtypeStruct((-(-sum(one[2] for one in blocks) // 16) * 16, 128), BF) for blocks in plan]
    return run(
        functools.partial(pack_kernel, plan),
        "pack",
        order,
        deps,
        inputs,
        [whole_spec(one.shape) for one in inputs],
        [whole_spec(one.shape) for one in shapes],
        shapes,
        (),
        (1,),
        cost(0, sum(4 * one.size for one in inputs)),
    )


def pack_plans(share, width, hidden):
    triple = [(0, 0, share, 128 * at, 128) for at in range(3 * width // 128)]
    triple += [(at, 0, 1, 0, share) for at in range(1, 7)] + [(7, 0, 1, at * share, share) for at in range(2)]
    triple += [(8, 0, 1, at * 128, 128) for at in range(hidden // PARTS // 128)]
    others = [(0, 0, share, 128 * at, 128) for at in range(width // 128)]
    others += [(1, 0, share, 128 * at, 128) for at in range(hidden // 128)]
    others += [(2, 0, hidden // PARTS, 128 * at, 128) for at in range(width // 128)]
    return [triple], [others]


def scatter(part):
    return lax.psum(lax.psum_scatter(part, "shard", scatter_dimension=0, tiled=True), "rep")


def diagonal(even, got, start, rows):
    return (rows, (even, 3, start), (got, 3, start))


def total(even, got, from_x, from_y, start, base, rows):
    return (rows, (even, 0, start), (got, 0, start), (from_x, None, base), (from_y, None, base))


def relay(lists, from_x, from_y, cut):
    outs = []
    for index, brought, upper in ((1, from_y, False), (2, from_x, True)):
        segments, first = [], 0
        for even, got, rows in lists:
            last = first + rows
            for start, stop in ((first, min(last, cut)), (max(first, cut), last)):
                if start >= stop:
                    continue
                terms = [(even, index, start - first), (got, index, start - first)]
                if (start < cut) == upper:
                    terms.append((brought, None, start if upper else start - cut))
                segments.append((stop - start, *terms))
            first = last
        outs.append(segments)
    return outs


def shards(
    count,
    tokens,
    segments,
    cotangent,
    attend_gain,
    attend_shift,
    triple_weight,
    triple_bias,
    output_weight,
    output_bias,
    feed_gain,
    feed_shift,
    expand_weight,
    expand_bias,
    reduce_weight,
    reduce_bias,
):
    rows, width = tokens.shape
    hidden = expand_weight.shape[1]
    share = width // PARTS
    small = (attend_gain, attend_shift, output_bias, feed_gain, feed_shift, reduce_bias, triple_bias, expand_bias)
    plan_a, plan_b = pack_plans(share, width, hidden)
    local = count == PARTS and lax.axis_size("rep") == 4
    if local:
        order = jnp.stack([lax.axis_index("shard"), lax.axis_index("rep")]).astype(jnp.int32)
        small = [one.reshape(1, -1) for one in small]
        (own_a,) = pack_parts(order, (), (triple_weight, *small), plan_a)
        x_a, y_a, c_a = swap(own_a, 2), swap(own_a, 4), swap(own_a, 1)
        cut_a = 9 * share
        send_y, send_x = combine(
            order, (), [(cut_a, (x_a, None, 0))], [(own_a.shape[0] - cut_a, (y_a, None, cut_a))]
        )
        u_a, l_a = swap(send_y, 4), swap(send_x, 2)
        pack_a = (own_a, c_a, x_a, swap(x_a, 1), y_a, swap(y_a, 1), u_a, l_a, swap(u_a, 1), swap(l_a, 1))
        (own_b,) = pack_parts(order, (send_y,), (output_weight, expand_weight, reduce_weight), plan_b)
        x_b, y_b, c_b = swap(own_b, 2), swap(own_b, 4), swap(own_b, 1)
    else:
        order = jnp.zeros((2,), jnp.int32)
        weights = (triple_weight, output_weight, expand_weight, reduce_weight, small)
        weights = jax.tree.map(lambda one: lax.all_gather(one, "shard", axis=0, tiled=True), weights)
        weights = jax.tree.map(lambda one: one.reshape(PARTS, -1, *one.shape[1:]), weights)
        pack_a, pack_b = [], []
        for part in range(PARTS):
            vectors = [one[part : part + 1] for one in weights[4]]
            pack_a += pack_parts(order, (), (weights[0][part], *vectors), plan_a)
            pack_b += pack_parts(order, (), [one[part] for one in weights[1:4]], plan_b)
    col = segments.reshape(rows, 1)
    row = segments.reshape(1, rows)

    qkv, turned_one, vectors, bias_up = project(order, (own_b,) if local else (), pack_a, tokens, hidden)
    mixed, logs = [None] * HALVES, [None] * HALVES
    mixed[0], logs[0] = attend_forward(order, (), col, row, qkv, 0)
    mixed[1], logs[1] = attend_forward(order, (mixed[0],), col, row, qkv, 1)
    deps = (mixed[1],)
    if local:
        cut_b = own_b.shape[0] // 2
        send_y, send_x = combine(
            order, deps, [(cut_b, (x_b, None, 0))], [(own_b.shape[0] - cut_b, (y_b, None, cut_b))]
        )
        u_b, l_b = swap(send_y, 4), swap(send_x, 2)
        x_b, y_b = gate((send_y,), x_b, y_b)
        c_x_b, c_y_b = swap(x_b, 1), swap(y_b, 1)
        deps = (x_b,)
    mixed[2], logs[2] = attend_forward(order, deps, col, row, qkv, 2)
    if local:
        u_b, l_b = gate((mixed[2],), u_b, l_b)
        pack_b = (own_b, c_b, x_b, c_x_b, y_b, c_y_b, u_b, l_b, swap(u_b, 1), swap(l_b, 1))
    turned_two, feed, h, e, out_tokens, middle_grad, branch, mixed_grad, sums, wide = make_middle(
        order, (), pack_b, tokens, mixed, col, cotangent, vectors, bias_up
    )
    even_d, odd_d = down_grad(order, (), h, feed)
    deps = (even_d,)
    if local:
        got_d = swap(odd_d, 1)
    even_u, odd_u, even_o, odd_o = up_grad(order, deps, turned_two, e, branch, sums, wide, mixed)
    deps = (even_u,)
    rows_d, rows_u, rows_o = even_d.shape[1], even_u.shape[1], even_o.shape[1]
    if local:
        got_u, got_o = swap(odd_u, 1), swap(odd_o, 1)
        cut_d = rows_d // 2
        send_x, send_y = combine(
            order, deps, [diagonal(even_d, got_d, 0, cut_d)], [diagonal(even_d, got_d, cut_d, rows_d - cut_d)]
        )
        from_x, from_y = swap(send_x, 2), swap(send_y, 4)
        deps = (send_x,)
    grads = [attend_backward(order, deps, col, row, qkv, mixed[0], logs[0], mixed_grad, 0)]
    deps = (grads[0],)
    if local:
        cut_u = (rows_u + rows_o) // 32 * 16
        to_x, to_y, send_x, send_y = combine(
            order,
            deps,
            *relay([(even_d, got_d, rows_d)], from_x, from_y, cut_d),
            [diagonal(even_u, got_u, 0, cut_u)],
            [diagonal(even_u, got_u, cut_u, rows_u - cut_u), diagonal(even_o, got_o, 0, rows_o)],
        )
        down_x, down_y = swap(to_x, 2), swap(to_y, 4)
        from_x, from_y = swap(send_x, 2), swap(send_y, 4)
        deps = (to_x,)
    grads.append(attend_backward(order, deps, col, row, qkv, mixed[1], logs[1], mixed_grad, 1))
    even_a, odd_a, sum_a = triple_grad(order, (), turned_one, *grads)
    deps = (even_a,)
    rows_a = even_a.shape[1]
    if local:
        got_a = swap(odd_a, 1)
        half = rows_d // 2
        keep_d, send_d, to_x, to_y = combine(
            order,
            deps,
            [total(even_d, got_d, down_x, down_y, (0, half, False), (0, half, False), half)],
            [total(even_d, got_d, down_x, down_y, (0, half, True), (0, half, True), half)],
            *relay([(even_u, got_u, rows_u), (even_o, got_o, rows_o)], from_x, from_y, cut_u),
        )
        up_x, up_y = swap(to_x, 2), swap(to_y, 4)
        back_d = swap_rep(send_d, 1)
        deps = (keep_d,)
    grads.append(attend_backward(order, deps, col, row, qkv, mixed[2], logs[2], mixed_grad, 2))
    deps = (grads[2],)
    if local:
        cut_a = rows_a // 2
        keep_d, send_x, send_y = combine(
            order,
            deps,
            [(half, (keep_d, None, 0), (back_d, None, 0))],
            [diagonal(even_a, got_a, 0, cut_a)],
            [diagonal(even_a, got_a, cut_a, rows_a - cut_a)],
        )
        from_x, from_y = swap(send_x, 2), swap(send_y, 4)
        back_d = swap_rep(keep_d, 2)
        deps = (keep_d,)
    even_l, odd_l, grad_tokens = last_grads(
        order, deps, pack_a, tokens, turned_one, grads, middle_grad, vectors, sum_a
    )
    rows_l = even_l.shape[1]
    if local:
        got_l = swap(odd_l, 1)
        half_u, half_o = rows_u // 2, rows_o // 2
        keep_u, send_u, low, to_x, to_y = combine(
            order,
            (even_l,),
            [
                total(even_u, got_u, up_x, up_y, (0, half_u, False), (0, half_u, False), half_u),
                total(even_o, got_o, up_x, up_y, (0, half_o, False), (rows_u, half_o, False), half_o),
            ],
            [
                total(even_u, got_u, up_x, up_y, (0, half_u, True), (0, half_u, True), half_u),
                total(even_o, got_o, up_x, up_y, (0, half_o, True), (rows_u, half_o, True), half_o),
            ],
            [(half, (keep_d, None, 0), (back_d, None, 0))],
            *relay([(even_a, got_a, rows_a)], from_x, from_y, cut_a),
        )
        far_x, far_y = swap(to_x, 2), swap(to_y, 4)
        cut_l = rows_l // 32 * 16
        send_x, send_y = combine(
            order,
            (to_x,),
            [diagonal(even_l, got_l, 0, cut_l)],
            [diagonal(even_l, got_l, cut_l, rows_l - cut_l)],
        )
        from_x, from_y = swap(send_x, 2), swap(send_y, 4)
        back_u, low_other = swap_rep(send_u, 1), swap_rep(low, 1)
        to_x, to_y = combine(order, (), *relay([(even_l, got_l, rows_l)], from_x, from_y, cut_l))
        last_x, last_y = swap(to_x, 2), swap(to_y, 4)
        keep_u, sum_a = combine(
            order,
            (to_x,),
            [(half_u + half_o, (keep_u, None, 0), (back_u, None, 0))],
            [total(even_a, got_a, far_x, far_y, 0, 0, rows_a)],
        )
        back_a, back_u = swap_rep(sum_a, 1), swap_rep(keep_u, 2)
        (sum_l,) = combine(order, (sum_a,), [total(even_l, got_l, last_x, last_y, 0, 0, rows_l)])
        back_l = swap_rep(sum_l, 1)
        (sum_a,) = combine(order, (sum_l,), [(rows_a, (sum_a, None, 0), (back_a, None, 0))])
        back_a = swap_rep(sum_a, 2)
        (sum_l,) = combine(order, (sum_a,), [(rows_l, (sum_l, None, 0), (back_l, None, 0))])
        back_l = swap_rep(sum_l, 2)
        (keep_u,) = combine(
            order, (sum_l,), [(half_u + half_o, (keep_u, None, 0), (back_u, None, 0))]
        )
        back_u = swap_rep(keep_u, 1)
        grad_triple, late = triple_owner(order, (keep_u,), width, sum_a, back_a, sum_l, back_l)
        grad_expand, grad_reduce, grad_output, early = owner_parts(
            order, (grad_triple,), width, hidden, keep_u, back_u, low, low_other
        )
    else:
        def natural(even, odd):
            return [(odd if at % 2 else even)[at // 2] for at in range(PARTS)]

        parts = [natural(*one) for one in ((even_u, odd_u), (even_o, odd_o), (even_d, odd_d), (even_a, odd_a), (even_l, odd_l))]
        found = []
        for up, out, down, first, last in zip(*parts):
            halves = [
                jnp.concatenate([up[at * (rows_u // 2) : (at + 1) * (rows_u // 2)], out[at * (rows_o // 2) : (at + 1) * (rows_o // 2)]])
                for at in range(2)
            ]
            one = owner_parts(order, (), width, hidden, *halves, down[: rows_d // 2], down[rows_d // 2 :])
            found.append((*one, *triple_owner(order, (), width, first, jnp.zeros_like(first), last, jnp.zeros_like(last))))
        grad_expand, grad_reduce, grad_output, early, grad_triple, late = [list(one) for one in zip(*found)]
        grad_expand, grad_reduce, grad_output, grad_triple = [
            scatter(jnp.concatenate(one).astype(BF)).astype(F32)
            for one in (grad_expand, grad_reduce, grad_output, grad_triple)
        ]

    def one_vector(at):
        source, first, last, columns = (
            (late, 0, 1, share),
            (late, 1, 2, share),
            (late, 2, 4, share),
            (early, 2, 3, share),
            (early, 0, 1, share),
            (early, 1, 2, share),
            (early, 4, 4 + hidden // PARTS // 128, 128),
            (early, 3, 4, share),
        )[at]
        if local:
            return source[first:last, :columns].reshape(-1)
        whole = jnp.concatenate([one[first:last, :columns].reshape(-1) for one in source])
        return scatter(whole.astype(BF)).astype(F32)

    return (
        out_tokens,
        grad_tokens,
        one_vector(0),
        one_vector(1),
        grad_triple,
        one_vector(2),
        grad_output,
        one_vector(3),
        one_vector(4),
        one_vector(5),
        grad_expand,
        one_vector(6),
        grad_reduce,
        one_vector(7),
    )


def solution(mesh):
    return jax.shard_map(
        functools.partial(shards, mesh.shape["shard"]),
        mesh=mesh,
        in_specs=(
            P(("shard", "rep"), None),
            P(("shard", "rep")),
            P(("shard", "rep"), None),
            P("shard"),
            P("shard"),
            P("shard", None),
            P("shard"),
            P("shard", None),
            P("shard"),
            P("shard"),
            P("shard"),
            P("shard", None),
            P("shard"),
            P("shard", None),
            P("shard"),
        ),
        out_specs=(
            P(("shard", "rep"), None),
            P(("shard", "rep"), None),
            P("shard"),
            P("shard"),
            P("shard", None),
            P("shard"),
            P("shard", None),
            P("shard"),
            P("shard"),
            P("shard"),
            P("shard", None),
            P("shard"),
            P("shard", None),
            P("shard"),
        ),
        check_vma=False,
    )
```

```python
import functools

import jax
import jax.numpy as jnp
from jax import lax
from jax.experimental import pallas as pl
from jax.experimental.pallas import tpu as pltpu
from jax.sharding import PartitionSpec as P

HEAD_DIM = 64
PARTS = 8
HALVES = 3
GAIN_ONE, SHIFT_ONE, BIAS_OUT, GAIN_TWO, SHIFT_TWO, BIAS_DOWN, BIAS_QV = range(7)
VECTOR_ROWS = ((0,), (1,), (2,), (3,), (4,), (5,), (6, 7))
EPSILON = 1e-05
BF = jnp.bfloat16
F32 = jnp.float32
NEVER = -1e30
ROOT = 0.7978845608028654
MIB = 1 << 20
VMEM = 60


def dot_nn(left, right):
    return lax.dot_general(left, right, (((1,), (0,)), ((), ())), preferred_element_type=F32)


def dot_nt(left, right):
    return lax.dot_general(left, right, (((1,), (1,)), ((), ())), preferred_element_type=F32)


def dot_tn(left, right):
    return lax.dot_general(left, right, (((0,), (0,)), ((), ())), preferred_element_type=F32)


def normalise(values):
    center = values - jnp.mean(values, axis=-1, keepdims=True)
    variance = jnp.mean(center * center, axis=-1, keepdims=True)
    scale = lax.rsqrt(variance + EPSILON)
    return center * scale, scale


def norm_back(values, incoming, gain):
    unit, scale = normalise(values)
    scaled = incoming * gain
    first = jnp.mean(scaled, axis=-1, keepdims=True)
    second = jnp.mean(scaled * unit, axis=-1, keepdims=True)
    back = scale * (scaled - first - unit * second)
    return back, jnp.sum(incoming * unit, axis=0, keepdims=True)


def whole_spec(shape):
    return pl.BlockSpec(shape, lambda *_: (0,) * len(shape))


def once_spec(shape):
    return pl.BlockSpec(shape, lambda *_: (0,) * len(shape), pipeline_mode=pl.Buffered(1))


def cost(flops, moved, exps=0):
    return pl.CostEstimate(flops=int(flops), bytes_accessed=int(moved), transcendentals=int(exps))


def run(
    kernel, name, order, deps, inputs, in_specs, out_specs, out_shape, scratch=(), grid=(1,), estimate=None, vmem=VMEM
):
    count = len(deps)

    def body(order_ref, *refs):
        kernel(order_ref, *refs[count:])

    return pl.pallas_call(
        body,
        grid_spec=pltpu.PrefetchScalarGridSpec(
            num_scalar_prefetch=1,
            grid=grid,
            in_specs=[pl.BlockSpec(memory_space=pl.ANY)] * count + list(in_specs),
            out_specs=out_specs,
            scratch_shapes=list(scratch),
        ),
        out_shape=out_shape,
        compiler_params=pltpu.CompilerParams(vmem_limit_bytes=vmem * MIB),
        cost_estimate=estimate,
        name=name,
    )(order, *deps, *inputs)


def gate(deps, *values):
    count, size = len(deps), len(values)
    return pl.pallas_call(
        lambda *_: None,
        in_specs=[pl.BlockSpec(memory_space=pl.ANY)] * (count + size),
        out_specs=[pl.BlockSpec(memory_space=pl.ANY)] * size,
        out_shape=[jax.ShapeDtypeStruct(one.shape, one.dtype) for one in values],
        input_output_aliases={count + at: at for at in range(size)},
        name="gate",
    )(*deps, *values)


def fill_weight(order_ref, pieces, first, blocks, out_ref, rows, lead=None):
    mine = order_ref[0]
    for piece in range(PARTS):
        place = pl.ds(pl.multiple_of((piece ^ mine) * rows, 32), rows)
        for at in range(blocks):
            tile = piece_rows(pieces, piece, first + at * rows, rows)
            if lead is None:
                out_ref[place, at * 128 : (at + 1) * 128] = tile
            else:
                group, inside = divmod(at, lead)
                out_ref[group, place, inside * 128 : (inside + 1) * 128] = tile


def piece_rows(pieces, piece, start, rows):
    if len(pieces) == PARTS or piece < 6:
        return pieces[piece][start : start + rows, :]
    cut = pieces[6].shape[0]
    if start < cut:
        return pieces[2 * piece - 6][start : start + rows, :]
    return pieces[2 * piece - 5][start - cut : start - cut + rows, :]


def put_pieces(order_ref, even_ref, odd_ref, place, value):
    chip = lax.shift_right_logical(order_ref[0], 1)
    for core in range(2):
        @pl.when(lax.rem(order_ref[0], 2) == core)
        def _():
            for part in range(PARTS):
                out_ref = even_ref if part % 2 == core else odd_ref
                out_ref[(part // 2) ^ chip, place, :] = value(part)


def project_kernel(width, count, order_ref, *refs):
    pieces, (x_ref, qkv_ref, turned_ref, vector_ref, up_ref, w_ref, v_ref) = refs[:count], refs[count:]
    share = width // PARTS

    @pl.when(pl.program_id(0) == 0)
    def _():
        fill_weight(order_ref, pieces, 0, 3 * width // 128, w_ref, share, width // 128)
        for piece in range(PARTS):
            v_ref[piece ^ order_ref[0]] = piece_rows(pieces, piece, 3 * width // 128 * share, 16).astype(F32)
        vector_ref[...] = jnp.zeros_like(vector_ref)
        for out, places in enumerate(VECTOR_ROWS):
            parts = [
                v_ref[at // len(places), places[at % len(places)] : places[at % len(places)] + 1, :share]
                for at in range(PARTS * len(places))
            ]
            for at in range(len(places)):
                row = jnp.concatenate(parts[at * PARTS : (at + 1) * PARTS], axis=1)
                vector_ref[out + at : out + at + 1, :] = row
        wide = up_ref.shape[1] // PARTS // 128
        for part in range(PARTS):
            for at in range(wide):
                first = (part * wide + at) * 128
                up_ref[:, first : first + 128] = v_ref[part, 8 + at : 9 + at, :]

    unit, _ = normalise(x_ref[...].astype(F32))
    normed = (unit * vector_ref[GAIN_ONE : GAIN_ONE + 1, :] + vector_ref[SHIFT_ONE : SHIFT_ONE + 1, :]).astype(BF)
    turned_ref[...] = normed.T
    for at in range(3):
        product = dot_nn(normed, w_ref[at])
        if at != 1:
            product = product + vector_ref[BIAS_QV + at // 2 : BIAS_QV + at // 2 + 1, :]
        qkv_ref[at] = product.astype(BF)


def project(order, deps, pack, x, hidden):
    rows, width = x.shape
    block = min(256, rows)
    return run(
        functools.partial(project_kernel, width, len(pack)),
        "project",
        order,
        deps,
        (*pack, x),
        [whole_spec(one.shape) for one in pack] + [pl.BlockSpec((block, width), lambda i, *_: (i, 0))],
        [
            pl.BlockSpec((3, block, width), lambda i, *_: (0, i, 0)),
            pl.BlockSpec((width, block), lambda i, *_: (0, i)),
            whole_spec((8, width)),
            whole_spec((1, hidden)),
        ],
        [
            jax.ShapeDtypeStruct((3, rows, width), BF),
            jax.ShapeDtypeStruct((width, rows), BF),
            jax.ShapeDtypeStruct((8, width), F32),
            jax.ShapeDtypeStruct((1, hidden), F32),
        ],
        [pltpu.VMEM((3, width, width), BF), pltpu.VMEM((PARTS, 16, 128), F32)],
        (rows // block,),
        cost(6 * rows * width * width, 14 * rows * width),
    )


def attend_forward_kernel(block, order_ref, col_ref, row_ref, qkv_ref, mixed_ref, log_ref, bias_ref):
    rows = row_ref.shape[1]

    @pl.when(pl.program_id(0) == 0)
    def _():
        for first in range(0, rows, block):
            at = lax.broadcasted_iota(jnp.int32, (block, rows), 0) + first
            key = lax.broadcasted_iota(jnp.int32, (block, rows), 1)
            same = col_ref[first : first + block, :] == row_ref[...]
            bias_ref[first : first + block, :] = jnp.where(same & (key <= at), 0.0, NEVER)

    lane = lax.broadcasted_iota(jnp.int32, (block, 128), 1)
    for first in range(0, rows, block):
        last = first + block
        queries = qkv_ref[0, first:last, :] * jnp.asarray(0.125, BF)
        outs, logs = [], []
        for head in range(2):
            mine = (lane < HEAD_DIM) if head == 0 else (lane >= HEAD_DIM)
            scores = dot_nt(jnp.where(mine, queries, jnp.zeros_like(queries)), qkv_ref[1, :last, :])
            scores = scores + bias_ref[first:last, :last]
            largest = jnp.max(scores, axis=-1, keepdims=True)
            expo = jnp.exp(scores - largest)
            total = jnp.sum(expo, axis=-1, keepdims=True)
            outs.append(dot_nn(expo.astype(BF), qkv_ref[2, :last, :]) / total)
            logs.append(largest + jnp.log(total))
        mixed_ref[first:last, :] = jnp.where(lane < HEAD_DIM, outs[0], outs[1]).astype(BF)
        log_ref[0, first:last, :] = jnp.where(lane < HEAD_DIM, logs[1], logs[0])


def attend_forward(order, deps, col, row, qkv, half):
    _, rows, width = qkv.shape
    pairs = width // 128 // HALVES
    block = min(256, rows)
    return run(
        functools.partial(attend_forward_kernel, block),
        "attend_forward",
        order,
        deps,
        (col, row, qkv),
        [
            whole_spec(col.shape),
            whole_spec(row.shape),
            pl.BlockSpec((3, rows, 128), lambda i, *_: (0, 0, i + half * pairs)),
        ],
        [
            pl.BlockSpec((rows, 128), lambda i, *_: (0, i)),
            pl.BlockSpec((1, rows, 128), lambda i, *_: (i, 0, 0)),
        ],
        [
            jax.ShapeDtypeStruct((rows, width // HALVES), BF),
            jax.ShapeDtypeStruct((pairs, rows, 128), F32),
        ],
        [pltpu.VMEM((rows, rows), F32)],
        (pairs,),
        cost(8 * rows * rows * width, 6 * rows * width, rows * rows * pairs),
    )


def split_lanes(value, lane):
    high = value.astype(BF)
    rest = value - high.astype(F32)
    middle = rest.astype(BF)
    low = (rest - middle.astype(F32)).astype(BF)
    inside = lax.rem(lane, HEAD_DIM)
    zero = jnp.zeros_like(high)
    return jnp.where(inside == 0, high, jnp.where(inside == 1, middle, jnp.where(inside == 2, low, zero)))


def attend_backward_kernel(
    block, order_ref, col_ref, row_ref, qkv_ref, mixed_ref, log_ref, grad_ref, out_ref, bias_ref, q_ref, k_ref, d_ref, v_ref,
    dq_ref,
):
    rows = row_ref.shape[1]

    @pl.when(pl.program_id(0) == 0)
    def _():
        for first in range(0, rows, block):
            key = lax.broadcasted_iota(jnp.int32, (block, rows), 0) + first
            at = lax.broadcasted_iota(jnp.int32, (block, rows), 1)
            same = col_ref[first : first + block, :] == row_ref[...]
            bias_ref[first : first + block, :] = jnp.where(same & (key <= at), 0.0, NEVER)

    lane = lax.broadcasted_iota(jnp.int32, (block, 128), 1)
    below = lane < HEAD_DIM
    minus = jnp.where(lax.rem(lane, HEAD_DIM) < 3, -1.0, 0.0).astype(BF)
    for first in range(0, rows, block):
        last = first + block
        queries = qkv_ref[0, first:last, :] * jnp.asarray(0.125, BF)
        keys = qkv_ref[1, first:last, :]
        values = qkv_ref[2, first:last, :]
        grads = grad_ref[first:last, :]
        product = grads.astype(F32) * mixed_ref[first:last, :].astype(F32)
        sums = [
            jnp.sum(jnp.where(below, product, 0.0), axis=-1, keepdims=True),
            jnp.sum(jnp.where(below, 0.0, product), axis=-1, keepdims=True),
        ]
        logs = split_lanes(log_ref[0, first:last, :], lane)
        inner = split_lanes(jnp.where(below, sums[1], sums[0]), lane)
        for head in range(2):
            mine = below if head == 0 else lane >= HEAD_DIM
            q_ref[head, first:last, :] = jnp.where(mine, queries, logs)
            k_ref[head, first:last, :] = jnp.where(mine, keys, minus)
            d_ref[head, first:last, :] = jnp.where(mine, grads, inner)
            v_ref[head, first:last, :] = jnp.where(mine, values, minus)

    for first in range(0, rows, block):
        last = first + block
        key_parts, value_parts, query_parts = [], [], []
        for head in range(2):
            scores = dot_nt(k_ref[head, first:last, :], q_ref[head, first:, :]) + bias_ref[first:last, first:]
            probs = jnp.exp(scores)
            slopes = probs * dot_nt(v_ref[head, first:last, :], d_ref[head, first:, :])
            slopes = slopes.astype(BF)
            value_parts.append(dot_nn(probs.astype(BF), d_ref[head, first:, :]))
            key_parts.append(dot_nn(slopes, q_ref[head, first:, :]))
            query_parts.append(dot_tn(slopes, k_ref[head, first:last, :]))
        out_ref[1, first:last, :] = jnp.where(below, key_parts[0], key_parts[1]).astype(BF)
        out_ref[2, first:last, :] = jnp.where(below, value_parts[0], value_parts[1]).astype(BF)
        side = lax.broadcasted_iota(jnp.int32, (rows - first, 128), 1) < HEAD_DIM
        part = jnp.where(side, query_parts[0], query_parts[1])
        if first == 0:
            dq_ref[...] = part
        else:
            dq_ref[first:, :] += part
    out_ref[0] = (dq_ref[...] * 0.125).astype(BF)


def attend_backward(order, deps, col, row, qkv, mixed, log_total, grad, half):
    _, rows, width = qkv.shape
    pairs = width // 128 // HALVES
    block = min(256, rows)
    return run(
        functools.partial(attend_backward_kernel, block),
        "attend_backward",
        order,
        deps,
        (col, row, qkv, mixed, log_total, grad),
        [
            whole_spec(col.shape),
            whole_spec(row.shape),
            pl.BlockSpec((3, rows, 128), lambda i, *_: (0, 0, i + half * pairs)),
            pl.BlockSpec((rows, 128), lambda i, *_: (0, i)),
            pl.BlockSpec((1, rows, 128), lambda i, *_: (i, 0, 0)),
            pl.BlockSpec((rows, 128), lambda i, *_: (0, i + half * pairs)),
        ],
        pl.BlockSpec((3, rows, 128), lambda i, *_: (0, 0, i)),
        jax.ShapeDtypeStruct((3, rows, width // HALVES), BF),
        [pltpu.VMEM((rows, rows), F32)] + [pltpu.VMEM((2, rows, 128), BF)] * 4 + [pltpu.VMEM((rows, 128), F32)],
        (pairs,),
        cost(20 * rows * rows * width, 10 * rows * width, rows * rows * pairs),
    )


def middle_kernel(width, hidden, steps, count, order_ref, *refs):
    pieces, refs = refs[:count], refs[count:]
    x_ref, seg_ref, cot_ref, vector_ref, bias_ref, *refs = refs
    mixed_refs, refs = refs[:HALVES], refs[HALVES:]
    turned_ref, feed_ref, h_ref, e_ref, out_ref, grad_ref, branch_ref, mixed_grad_ref, sums_ref, wide_ref, *refs = refs
    wo_ref, we_ref, wr_ref = refs
    share = width // PARTS

    @pl.when(pl.program_id(0) == 0)
    def _():
        fill_weight(order_ref, pieces, 0, width // 128, wo_ref, share)
        fill_weight(order_ref, pieces, width // 128 * share, hidden // 128, we_ref, share)
        fill_weight(order_ref, pieces, (width + hidden) // 128 * share, width // 128, wr_ref, hidden // PARTS)
        sums_ref[...] = jnp.zeros_like(sums_ref)
        wide_ref[...] = jnp.zeros_like(wide_ref)

    def vector(at):
        return vector_ref[at : at + 1, :]

    mixed = jnp.concatenate([one[...] for one in mixed_refs], axis=1)
    middle = x_ref[...].astype(F32) + dot_nn(mixed, wo_ref[...]) + vector(BIAS_OUT)
    unit, scale = normalise(middle)
    normed = (unit * vector(GAIN_TWO) + vector(SHIFT_TWO)).astype(BF)
    turned_ref[...] = normed.T
    live = seg_ref[...] >= 0
    feed = jnp.where(live, cot_ref[...].astype(F32), 0.0)
    feed_low = feed.astype(BF)
    feed_ref[...] = feed_low
    for at in range(0, hidden, 256):
        cols = slice(at, at + 256)
        u = dot_nn(normed, we_ref[:, cols]) + bias_ref[:, cols]
        hidden_grad = dot_nt(feed_low, wr_ref[cols, :])
        square = u * u
        tanh = jnp.tanh(u * (ROOT + (ROOT * 0.044715) * square))
        half = 0.5 + 0.5 * tanh
        h_ref[:, cols] = (u * half).astype(BF)
        slope = half + u * (0.5 - 0.5 * (tanh * tanh)) * (ROOT + (3 * 0.044715 * ROOT) * square)
        e_part = (hidden_grad * slope).astype(BF)
        e_ref[:, cols] = e_part
        wide_ref[:, cols] += jnp.sum(e_part.astype(F32), axis=0, keepdims=True)
    total = middle + dot_nn(h_ref[...], wr_ref[...]) + vector(BIAS_DOWN)
    out_ref[...] = jnp.where(live, total, 0.0).astype(BF)
    back = dot_nt(e_ref[...], we_ref[...])
    scaled = back * vector(GAIN_TWO)
    mean = jnp.mean(scaled, axis=-1, keepdims=True)
    second = jnp.mean(scaled * unit, axis=-1, keepdims=True)
    grad = feed + scale * (scaled - mean - unit * second)
    grad_ref[...] = grad
    branch = grad.astype(BF)
    branch_ref[...] = branch
    mixed_grad_ref[...] = dot_nt(branch, wo_ref[...]).astype(BF)
    sums_ref[0:1, :] += jnp.sum(back * unit, axis=0, keepdims=True)
    sums_ref[1:2, :] += jnp.sum(back, axis=0, keepdims=True)
    sums_ref[2:3, :] += jnp.sum(branch.astype(F32), axis=0, keepdims=True)
    sums_ref[3:4, :] += jnp.sum(feed, axis=0, keepdims=True)


def make_middle(order, deps, pack, x, mixed, col, cot, vectors, bias):
    rows, width = x.shape
    hidden = bias.shape[1]
    block = min(256, rows)
    by_rows = pl.BlockSpec((block, width), lambda i, *_: (i, 0))
    by_wide = pl.BlockSpec((block, hidden), lambda i, *_: (i, 0))
    low = jax.ShapeDtypeStruct((rows, width), BF)
    return run(
        functools.partial(middle_kernel, width, hidden, rows // block, len(pack)),
        "middle",
        order,
        deps,
        (*pack, x, col, cot, vectors, bias, *mixed),
        [once_spec(one.shape) for one in pack]
        + [by_rows, pl.BlockSpec((block, 1), lambda i, *_: (i, 0)), by_rows]
        + [whole_spec(vectors.shape), whole_spec(bias.shape)]
        + [pl.BlockSpec((block, width // HALVES), lambda i, *_: (i, 0))] * HALVES,
        [pl.BlockSpec((width, block), lambda i, *_: (0, i)), by_rows, by_wide, by_wide]
        + [by_rows] * 4
        + [whole_spec((8, width)), whole_spec((1, hidden))],
        [
            jax.ShapeDtypeStruct((width, rows), BF),
            low,
            jax.ShapeDtypeStruct((rows, hidden), BF),
            jax.ShapeDtypeStruct((rows, hidden), BF),
            low,
            jax.ShapeDtypeStruct((rows, width), F32),
            low,
            low,
            jax.ShapeDtypeStruct((8, width), F32),
            jax.ShapeDtypeStruct((1, hidden), F32),
        ],
        [pltpu.VMEM((width, width), BF), pltpu.VMEM((width, hidden), BF), pltpu.VMEM((hidden, width), BF)],
        (rows // block,),
        cost(4 * rows * width * (width + 2 * hidden), 50 * rows * width, rows * hidden),
    )


def down_kernel(order_ref, h_ref, feed_ref, even_ref, odd_ref):
    grad = dot_tn(h_ref[...], feed_ref[...]).astype(BF)
    half, width = grad.shape[0] // 2, grad.shape[1]
    for core in range(2):
        @pl.when(lax.rem(order_ref[0], 2) == core)
        def _():
            for side in range(2):
                out_ref = even_ref if side == core else odd_ref
                for lane in range(width // 128):
                    out_ref[0, lane * half : (lane + 1) * half, :] = grad[
                        side * half : (side + 1) * half, lane * 128 : (lane + 1) * 128
                    ]


def down_grad(order, deps, h, feed):
    rows, hidden = h.shape
    width = feed.shape[1]
    pairs = PARTS // 2
    own = jax.ShapeDtypeStruct((pairs, hidden // PARTS * width // 128, 128), BF)
    own_spec = pl.BlockSpec((1, *own.shape[1:]), lambda i, order: (i ^ lax.shift_right_logical(order[0], 1), 0, 0))
    return run(
        down_kernel,
        "down_grad",
        order,
        deps,
        (h, feed),
        [pl.BlockSpec((rows, hidden // pairs), lambda i, *_: (0, i)), whole_spec(feed.shape)],
        [own_spec, own_spec],
        [own, own],
        (),
        (pairs,),
        cost(2 * rows * width * hidden, 4 * rows * hidden),
    )


def up_kernel(steps, order_ref, *refs):
    turned_ref, e_ref, branch_ref, sums_ref, wide_ref, *refs = refs
    mixed_refs, (even_ref, odd_ref, own_even_ref, own_odd_ref, t_ref) = refs[:HALVES], refs[HALVES:]
    step = pl.program_id(0)

    @pl.when(step < steps)
    def _():
        put_triple(order_ref, turned_ref[...], e_ref[...], even_ref, odd_ref, 0, False)

    @pl.when(step == steps)
    def _():
        width = branch_ref.shape[1]
        share, half = width // PARTS, width // 256
        third = width // HALVES
        for at, one in enumerate(mixed_refs):
            t_ref[at * third : (at + 1) * third, :] = dot_tn(one[...], branch_ref[...]).astype(BF)
        for lane in range(width // 128):
            base = lane * share + lane // half * 16
            put_pieces(
                order_ref, own_even_ref, own_odd_ref, slice(base, base + share),
                lambda part: t_ref[part * share : (part + 1) * share, lane * 128 : (lane + 1) * 128],
            )
        put_vectors(
            order_ref, own_even_ref, own_odd_ref, half * share, sums_ref,
            lambda part: [(at, part) for at in range(4)], wide_ref,
        )
        for one in (own_even_ref, own_odd_ref):
            one[:, 2 * half * share + 16 :, :] = jnp.zeros((PARTS // 2, 16, 128), BF)


def up_grad(order, deps, turned, e, branch, sums, wide, mixed):
    width, rows = turned.shape
    hidden = e.shape[1]
    steps = PARTS // 2
    share = width // PARTS
    part_rows = hidden // steps // 128 * share
    up = jax.ShapeDtypeStruct((PARTS // 2, hidden // 128 * share, 128), BF)
    own = jax.ShapeDtypeStruct((PARTS // 2, width // 128 * share + 32, 128), BF)
    up_spec = pl.BlockSpec((PARTS // 2, part_rows, 128), lambda i, *_: (0, jnp.minimum(i, steps - 1), 0))
    return run(
        functools.partial(up_kernel, steps),
        "up_grad",
        order,
        deps,
        (turned, e, branch, sums, wide, *mixed),
        [whole_spec(turned.shape), pl.BlockSpec((rows, hidden // steps), lambda i, *_: (0, jnp.minimum(i, steps - 1)))]
        + [whole_spec(one.shape) for one in (branch, sums, wide, *mixed)],
        [up_spec, up_spec, whole_spec(own.shape), whole_spec(own.shape)],
        [up, up, own, own],
        [pltpu.VMEM((width, width), BF)],
        (steps + 1,),
        cost(2 * rows * width * (hidden + width), 4 * rows * hidden),
    )


def put_vectors(order_ref, even_ref, odd_ref, base, sums_ref, shares, wide_ref=None):
    share = sums_ref.shape[1] // PARTS
    sums = sums_ref[...]
    blank = jnp.zeros((1, 128 - share), F32)

    def value(part):
        rows = [
            jnp.concatenate([sums[row : row + 1, at * share : (at + 1) * share], blank], axis=1)
            for row, at in shares(part)
        ]
        if wide_ref is not None:
            size = wide_ref.shape[1] // PARTS
            rows += [wide_ref[:, at : at + 128] for at in range(part * size, (part + 1) * size, 128)]
        rows.append(jnp.zeros((16 - len(rows), 128), F32))
        return jnp.concatenate(rows, axis=0).astype(BF)

    put_pieces(order_ref, even_ref, odd_ref, slice(base, base + 16), value)


def put_triple(order_ref, turned, grads, even_ref, odd_ref, base, summed=True):
    share = turned.shape[0] // PARTS
    product = dot_nn(turned, grads).astype(BF)
    for lane in range(grads.shape[1] // 128):
        put_pieces(
            order_ref, even_ref, odd_ref, pl.ds(base + lane * share, share),
            lambda part: product[part * share : (part + 1) * share, lane * 128 : (lane + 1) * 128],
        )
    return jnp.sum(grads.astype(F32), axis=0, keepdims=True) if summed else None


def triple_kernel(count, order_ref, turned_ref, *refs):
    grads, (even_ref, odd_ref, sum_ref) = refs[:count], refs[count:]
    part_rows = even_ref.shape[1] // count
    third = grads[0].shape[2]
    for at, one in enumerate(grads):
        sums = put_triple(order_ref, turned_ref[...], one[0], even_ref, odd_ref, at * part_rows)
        sum_ref[0, :, at * third : (at + 1) * third] = sums


def triple_grad(order, deps, turned, *grads):
    width, rows = turned.shape
    third, count = grads[0].shape[2], len(grads)
    part_rows = count * third // 128 * width // PARTS
    own = jax.ShapeDtypeStruct((PARTS // 2, 3 * part_rows, 128), BF)
    own_spec = pl.BlockSpec((PARTS // 2, part_rows, 128), lambda i, *_: (0, i, 0))
    by_third = pl.BlockSpec((1, rows, third), lambda i, *_: (i, 0, 0))
    return run(
        functools.partial(triple_kernel, count),
        "triple_grad",
        order,
        deps,
        (turned, *grads),
        [once_spec(turned.shape)] + [by_third] * count,
        [own_spec, own_spec, pl.BlockSpec((1, 1, count * third), lambda i, *_: (i, 0, 0))],
        [own, own, jax.ShapeDtypeStruct((3, 1, count * third), F32)],
        (),
        (3,),
        cost(6 * rows * width * third * count, 8 * rows * width),
    )


def input_kernel(width, steps, count, order_ref, *refs):
    pieces, refs = refs[:count], refs[count:]
    x_ref, *refs = refs
    third_refs, refs = refs[:HALVES], refs[HALVES:]
    middle_ref, vector_ref, sum_ref, late_ref, even_ref, odd_ref, out_ref, w_ref, sums_ref = refs
    step = pl.program_id(0)
    share, third = width // PARTS, width // HALVES

    @pl.when(step == 0)
    def _():
        fill_weight(order_ref, pieces, 0, 3 * width // 128, w_ref, share, width // 128)
        sums_ref[...] = jnp.zeros_like(sums_ref)

    back = None
    for at in range(3):
        one = dot_nt(jnp.concatenate([ref[at] for ref in third_refs], axis=1), w_ref[at])
        back = one if back is None else back + one
    part, gain_sum = norm_back(x_ref[...].astype(F32), back, vector_ref[GAIN_ONE : GAIN_ONE + 1, :])
    out_ref[...] = (middle_ref[...] + part).astype(BF)
    sums_ref[0:1, :] += gain_sum
    sums_ref[1:2, :] += jnp.sum(back, axis=0, keepdims=True)

    @pl.when(step == steps - 1)
    def _():
        for row, at in ((2, 0), (3, 2)):
            sums_ref[row : row + 1, : 2 * third] = sum_ref[at]
            sums_ref[row : row + 1, 2 * third :] = late_ref[at]
        put_vectors(
            order_ref, even_ref, odd_ref, 0, sums_ref,
            lambda part: [(0, part), (1, part)]
            + [(2 + at // PARTS, at % PARTS) for at in (2 * part, 2 * part + 1)],
        )


def input_grad(order, deps, pack, x, grads, middle_grad, vectors, sums, late):
    rows, width = x.shape
    third = width // HALVES
    block = min(512, rows)
    steps = rows // block
    own = jax.ShapeDtypeStruct((PARTS // 2, 16, 128), BF)
    by_rows = pl.BlockSpec((block, width), lambda i, *_: (i, 0))
    by_third = pl.BlockSpec((3, block, third), lambda i, *_: (0, i, 0))
    return run(
        functools.partial(input_kernel, width, steps, len(pack)),
        "input_grad",
        order,
        deps,
        (*pack, x, *grads, middle_grad, vectors, sums, late),
        [once_spec(one.shape) for one in pack]
        + [by_rows]
        + [by_third] * HALVES
        + [by_rows, whole_spec(vectors.shape), whole_spec(sums.shape), whole_spec(late.shape)],
        [whole_spec(own.shape), whole_spec(own.shape), by_rows],
        [own, own, jax.ShapeDtypeStruct((rows, width), BF)],
        [pltpu.VMEM((3, width, width), BF), pltpu.VMEM((8, width), F32)],
        (steps,),
        cost(6 * rows * width * width, 24 * rows * width),
    )


def owner_kernel(width, hidden, order_ref, mine_ref, other_ref, low_ref, low_other_ref, *outs):
    expand_ref, reduce_ref, output_ref, *vector_refs = outs
    share, tall, half = width // PARTS, hidden // PARTS, width // 256
    ups = hidden // 256
    bit = order_ref[1] & 1
    for place in range(2):
        @pl.when(bit == place)
        def _():
            for side in range(2):
                up_ref, down_ref = (mine_ref, low_ref) if side == place else (other_ref, low_other_ref)
                for at in range(ups):
                    first = (side * ups + at) * 128
                    expand_ref[:, first : first + 128] = up_ref[at * share : (at + 1) * share, :].astype(F32)
                base = ups * share
                for at in range(half):
                    first = (side * half + at) * 128
                    output_ref[:, first : first + 128] = up_ref[
                        base + at * share : base + (at + 1) * share, :
                    ].astype(F32)
                    reduce_ref[:, first : first + 128] = down_ref[at * tall : (at + 1) * tall, :].astype(F32)
                if side == 0:
                    vectors = up_ref[base + half * share : base + half * share + 16, :].astype(F32)
                    for at in range(4):
                        vector_refs[at][...] = vectors[at : at + 1, :share]
                    vector_refs[4][...] = vectors[4 : 4 + tall // 128, :]


def owner_parts(order, deps, width, hidden, mine, other, low, low_other):
    share, tall = width // PARTS, hidden // PARTS
    shapes = [(share, hidden), (tall, width), (share, width)] + [(1, share)] * 4 + [(tall // 128, 128)]
    return run(
        functools.partial(owner_kernel, width, hidden),
        "owner_parts",
        order,
        deps,
        (mine, other, low, low_other),
        [whole_spec(one.shape) for one in (mine, other, low, low_other)],
        [whole_spec(one) for one in shapes],
        [jax.ShapeDtypeStruct(one, F32) for one in shapes],
        (),
        (1,),
        cost(0, 6 * mine.size),
    )


def triple_owner_kernel(width, order_ref, mine_ref, other_ref, last_ref, more_ref, out_ref, *vector_refs):
    last = last_ref, more_ref
    share, tiles_each = width // PARTS, width // HALVES // 128
    tiles_half = 3 * tiles_each
    for place in range(2):
        @pl.when((order_ref[1] & 1) == place)
        def _():
            for index in range(2 * tiles_half):
                side, start = divmod(index, tiles_half)
                at, inside = divmod(index, 2 * tiles_each)
                column = (at * HALVES * tiles_each + inside) * 128
                ref = mine_ref if side == place else other_ref
                out_ref[:, column : column + 128] = ref[start * share : (start + 1) * share, :].astype(F32)
    for at in range(3):
        for tile in range(tiles_each):
            rows = slice((at * tiles_each + tile) * share, (at * tiles_each + tile + 1) * share)
            column = ((at * HALVES + 2) * tiles_each + tile) * 128
            out_ref[:, column : column + 128] = last[0][rows, :].astype(F32) + last[1][rows, :].astype(F32)
    rows = slice(3 * tiles_each * share, 3 * tiles_each * share + 16)
    vectors = last[0][rows, :].astype(F32) + last[1][rows, :].astype(F32)
    for at in range(4):
        vector_refs[at][...] = vectors[at : at + 1, :share]


def triple_owner(order, deps, width, *terms):
    shapes = [(width // PARTS, 3 * width)] + [(1, width // PARTS)] * 4
    return run(
        functools.partial(triple_owner_kernel, width),
        "triple_owner",
        order,
        deps,
        terms,
        [whole_spec(one.shape) for one in terms],
        [whole_spec(one) for one in shapes],
        [jax.ShapeDtypeStruct(one, F32) for one in shapes],
        (),
        (1,),
        cost(0, 12 * terms[0].size),
    )


def tiles(matrix):
    rows, cols = matrix.shape
    return matrix.reshape(rows, cols // 128, 128).transpose(1, 0, 2).reshape(-1, 128)


def untiles(packed, rows):
    return packed.reshape(-1, rows, 128).transpose(1, 0, 2).reshape(rows, -1)


def swap(value, mask):
    return lax.ppermute(value, "shard", [(at, at ^ mask) for at in range(PARTS)])


def swap_rep(value, mask):
    count = lax.axis_size("rep")
    return lax.ppermute(value, "rep", [(at, at ^ mask) for at in range(count)])


def combine_kernel(plan, order_ref, *refs):
    outs = refs[len(refs) - len(plan) :]
    for out_ref, segments in zip(outs, plan):
        at = 0
        for rows, terms in segments:
            total = None
            for source, start in terms:
                ref = refs[source]
                if isinstance(start, tuple):
                    base, half, flip = start
                    bit = order_ref[1] & 1
                    start = pl.multiple_of(base + (1 - bit if flip else bit) * half, 16)
                    rows_at = pl.ds(start, rows)
                else:
                    rows_at = slice(start, start + rows)
                one = ref[0, rows_at, :] if len(ref.shape) == 3 else ref[rows_at, :]
                if len(terms) > 1:
                    one = one.astype(F32)
                total = one if total is None else total + one
            out_ref[at : at + rows, :] = total.astype(BF)
            at += rows


def combine(order, deps, *outs):
    arrays, specs, places, plan, shapes = [], [], {}, [], []
    for segments in outs:
        steps = []
        for rows, *terms in segments:
            sources = []
            for array, index, start in terms:
                key = (id(array), index)
                if key not in places:
                    places[key] = len(arrays)
                    arrays.append(array)
                    if index is None:
                        specs.append(once_spec(array.shape))
                    else:
                        specs.append(pl.BlockSpec((1, *array.shape[1:]), lambda *_, index=index: (index, 0, 0),
                            pipeline_mode=pl.Buffered(1)))
                sources.append((places[key], start))
            steps.append((rows, tuple(sources)))
        plan.append(tuple(steps))
        shapes.append(jax.ShapeDtypeStruct((sum(rows for rows, _ in steps), 128), BF))
    moved = sum(2 * 128 * one.shape[-2] for one in arrays) + sum(256 * one.shape[0] for one in shapes)
    return run(
        functools.partial(combine_kernel, tuple(plan)),
        "combine",
        order,
        deps,
        arrays,
        specs,
        [whole_spec(one.shape) for one in shapes],
        shapes,
        (),
        (1,),
        cost(0, moved),
        24,
    )


def pack_kernel(plan, order_ref, *refs):
    outs = refs[len(refs) - len(plan) :]
    for out_ref, blocks in zip(outs, plan):
        at = 0
        for source, first, rows, column, columns in blocks:
            if rows == 1 and columns:
                if at % 16 == 0:
                    out_ref[at : at + 16, :] = jnp.zeros((16, 128), BF)
            out_ref[at : at + rows, :columns] = refs[source][first : first + rows, column : column + columns]
            at += rows


def pack_parts(order, deps, inputs, plan):
    shapes = [jax.ShapeDtypeStruct((-(-sum(one[2] for one in blocks) // 16) * 16, 128), BF) for blocks in plan]
    return run(
        functools.partial(pack_kernel, plan),
        "pack",
        order,
        deps,
        inputs,
        [whole_spec(one.shape) for one in inputs],
        [whole_spec(one.shape) for one in shapes],
        shapes,
        (),
        (1,),
        cost(0, sum(4 * one.size for one in inputs)),
    )


def pack_plans(share, width, hidden):
    triple = [(0, 0, share, 128 * at, 128) for at in range(3 * width // 128)]
    triple += [(at, 0, 1, 0, share) for at in range(1, 9)]
    triple += [(9, at, 1, 0, 128) for at in range(hidden // PARTS // 128)]
    others = [(0, 0, share, 128 * at, 128) for at in range(width // 128)]
    others += [(1, 0, share, 128 * at, 128) for at in range(hidden // 128)]
    others += [(2, 0, hidden // PARTS, 128 * at, 128) for at in range(width // 128)]
    return [triple], [others]


def vector_rows(share, small):
    *narrow, double, wide = small
    narrow += [double[:share], double[share:]]
    return [one.reshape(1, -1) for one in narrow] + [wide.reshape(-1, 128)]


def scatter(part):
    return lax.psum(lax.psum_scatter(part, "shard", scatter_dimension=0, tiled=True), "rep")


def diagonal(even, got, start, rows):
    return (rows, (even, 3, start), (got, 3, start))


def total(even, got, from_x, from_y, start, base, rows):
    return (rows, (even, 0, start), (got, 0, start), (from_x, None, base), (from_y, None, base))


def relay(lists, from_x, from_y, cut):
    outs = []
    for index, brought, upper in ((1, from_y, False), (2, from_x, True)):
        segments, first = [], 0
        for even, got, rows in lists:
            last = first + rows
            for start, stop in ((first, min(last, cut)), (max(first, cut), last)):
                if start >= stop:
                    continue
                terms = [(even, index, start - first), (got, index, start - first)]
                if (start < cut) == upper:
                    terms.append((brought, None, start if upper else start - cut))
                segments.append((stop - start, *terms))
            first = last
        outs.append(segments)
    return outs


def shards(
    count,
    tokens,
    segments,
    cotangent,
    attend_gain,
    attend_shift,
    triple_weight,
    triple_bias,
    output_weight,
    output_bias,
    feed_gain,
    feed_shift,
    expand_weight,
    expand_bias,
    reduce_weight,
    reduce_bias,
):
    rows, width = tokens.shape
    hidden = expand_weight.shape[1]
    share = width // PARTS
    small = (attend_gain, attend_shift, output_bias, feed_gain, feed_shift, reduce_bias, triple_bias, expand_bias)
    plan_a, plan_b = pack_plans(share, width, hidden)
    col = segments.reshape(rows, 1)
    row = segments.reshape(1, rows)
    local = count == PARTS and lax.axis_size("rep") == 4
    if local:
        order = jnp.stack([lax.axis_index("shard"), lax.axis_index("rep")]).astype(jnp.int32)
        (own_a,) = pack_parts(order, (), (triple_weight, *vector_rows(share, small)), plan_a)
        x_a, y_a, c_a = swap(own_a, 2), swap(own_a, 4), swap(own_a, 1)
        cut_a = 9 * share
        (own_b,) = pack_parts(order, (own_a, col), (output_weight, expand_weight, reduce_weight), plan_b)
        send_y, send_x = combine(
            order, (own_b, c_a), [(cut_a, (x_a, None, 0))], [(own_a.shape[0] - cut_a, (y_a, None, cut_a))]
        )
        u_a, l_a = swap(send_y, 4), swap(send_x, 2)
        pack_a = (own_a, c_a, x_a, swap(x_a, 1), y_a, swap(y_a, 1), u_a, l_a, swap(u_a, 1), swap(l_a, 1))
        (own_b,) = gate((send_y,), own_b)
        x_b, y_b = swap(own_b, 2), swap(own_b, 4)
    else:
        order = jnp.zeros((2,), jnp.int32)
        weights = (triple_weight, output_weight, expand_weight, reduce_weight, small)
        weights = jax.tree.map(lambda one: lax.all_gather(one, "shard", axis=0, tiled=True), weights)
        weights = jax.tree.map(lambda one: one.reshape(PARTS, -1, *one.shape[1:]), weights)
        pack_a, pack_b = [], []
        for part in range(PARTS):
            vectors = vector_rows(share, [one[part] for one in weights[4]])
            pack_a += pack_parts(order, (), (weights[0][part], *vectors), plan_a)
            pack_b += pack_parts(order, (), [one[part] for one in weights[1:4]], plan_b)
    qkv, turned_one, vectors, bias_up = project(order, (own_b,) if local else (), pack_a, tokens, hidden)
    mixed, logs = [None] * HALVES, [None] * HALVES
    mixed[0], logs[0] = attend_forward(order, (), col, row, qkv, 0)
    mixed[1], logs[1] = attend_forward(order, (mixed[0],), col, row, qkv, 1)
    deps = (mixed[1],)
    if local:
        cut_b = own_b.shape[0] // 2
        send_y, send_x = combine(
            order, deps, [(cut_b, (x_b, None, 0))], [(own_b.shape[0] - cut_b, (y_b, None, cut_b))]
        )
        u_b, l_b = swap(send_y, 4), swap(send_x, 2)
        x_b, y_b, own_b = gate((send_y,), x_b, y_b, own_b)
        c_b, c_x_b, c_y_b = swap(own_b, 1), swap(x_b, 1), swap(y_b, 1)
        deps = (x_b,)
    mixed[2], logs[2] = attend_forward(order, deps, col, row, qkv, 2)
    if local:
        u_b, l_b = gate((mixed[2],), u_b, l_b)
        pack_b = (own_b, c_b, x_b, c_x_b, y_b, c_y_b, u_b, l_b, swap(u_b, 1), swap(l_b, 1))
    turned_two, feed, h, e, out_tokens, middle_grad, branch, mixed_grad, sums, wide = make_middle(
        order, (), pack_b, tokens, mixed, col, cotangent, vectors, bias_up
    )
    even_d, odd_d = down_grad(order, (), h, feed)
    deps = (even_d,)
    if local:
        got_d = swap(odd_d, 1)
    even_u, odd_u, even_o, odd_o = up_grad(order, deps, turned_two, e, branch, sums, wide, mixed)
    deps = (even_u,)
    rows_d, rows_u, rows_o = even_d.shape[1], even_u.shape[1], even_o.shape[1]
    if local:
        got_u, got_o = swap(odd_u, 1), swap(odd_o, 1)
        cut_d = rows_d // 2
        send_x, send_y = combine(
            order, deps, [diagonal(even_d, got_d, 0, cut_d)], [diagonal(even_d, got_d, cut_d, rows_d - cut_d)]
        )
        from_x, from_y = swap(send_x, 2), swap(send_y, 4)
        deps = (send_x,)
    grads = [attend_backward(order, deps, col, row, qkv, mixed[0], logs[0], mixed_grad, 0)]
    deps = (grads[0],)
    if local:
        cut_u = (rows_u + rows_o) // 32 * 16
        to_x, to_y, send_x, send_y = combine(
            order,
            deps,
            *relay([(even_d, got_d, rows_d)], from_x, from_y, cut_d),
            [diagonal(even_u, got_u, 0, cut_u)],
            [diagonal(even_u, got_u, cut_u, rows_u - cut_u), diagonal(even_o, got_o, 0, rows_o)],
        )
        down_x, down_y = swap(to_x, 2), swap(to_y, 4)
        from_x, from_y = swap(send_x, 2), swap(send_y, 4)
        deps = (to_x,)
    grads.append(attend_backward(order, deps, col, row, qkv, mixed[1], logs[1], mixed_grad, 1))
    even_a, odd_a, sum_a = triple_grad(order, (), turned_one, *grads)
    deps = (even_a,)
    rows_a = even_a.shape[1]
    if local:
        got_a = swap(odd_a, 1)
        half = rows_d // 2
        keep_d, send_d, to_x, to_y = combine(
            order,
            deps,
            [total(even_d, got_d, down_x, down_y, (0, half, False), (0, half, False), half)],
            [total(even_d, got_d, down_x, down_y, (0, half, True), (0, half, True), half)],
            *relay([(even_u, got_u, rows_u), (even_o, got_o, rows_o)], from_x, from_y, cut_u),
        )
        up_x, up_y = swap(to_x, 2), swap(to_y, 4)
        back_d = swap_rep(send_d, 1)
        deps = (keep_d,)
    grads.append(attend_backward(order, deps, col, row, qkv, mixed[2], logs[2], mixed_grad, 2))
    deps = (grads[2],)
    if local:
        cut_a = rows_a // 2
        half_u, half_o = rows_u // 2, rows_o // 2
        keep_d, keep_u, send_u, send_x, send_y = combine(
            order,
            deps,
            [(half, (keep_d, None, 0), (back_d, None, 0))],
            [
                total(even_u, got_u, up_x, up_y, (0, half_u, False), (0, half_u, False), half_u),
                total(even_o, got_o, up_x, up_y, (0, half_o, False), (rows_u, half_o, False), half_o),
            ],
            [
                total(even_u, got_u, up_x, up_y, (0, half_u, True), (0, half_u, True), half_u),
                total(even_o, got_o, up_x, up_y, (0, half_o, True), (rows_u, half_o, True), half_o),
            ],
            [diagonal(even_a, got_a, 0, cut_a)],
            [diagonal(even_a, got_a, cut_a, rows_a - cut_a)],
        )
        from_x, from_y = swap(send_x, 2), swap(send_y, 4)
        back_d, back_u = swap_rep(keep_d, 2), swap_rep(send_u, 1)
        deps = (keep_d,)
    even_l, odd_l, late = triple_grad(order, deps, turned_one, grads[2])
    rows_l, rows_v = even_l.shape[1], 16
    deps = (even_l,)
    if local:
        keep_u, to_x, to_y = combine(
            order,
            deps,
            [(half_u + half_o, (keep_u, None, 0), (back_u, None, 0))],
            *relay([(even_a, got_a, rows_a)], from_x, from_y, cut_a),
        )
        far_x, far_y = swap(to_x, 2), swap(to_y, 4)
        back_u = swap_rep(keep_u, 2)
        deps = (to_x,)
        (odd_l,) = gate(deps, odd_l)
        got_l = swap(odd_l, 1)
    even_v, odd_v, grad_tokens = input_grad(
        order, deps, pack_a, tokens, grads, middle_grad, vectors, sum_a, late
    )
    if local:
        half_a = rows_a // 2
        keep_a, send_a, low = combine(
            order,
            (even_v,),
            [total(even_a, got_a, far_x, far_y, (0, half_a, False), (0, half_a, False), half_a)],
            [total(even_a, got_a, far_x, far_y, (0, half_a, True), (0, half_a, True), half_a)],
            [(half, (keep_d, None, 0), (back_d, None, 0))],
        )
        (odd_v,) = gate((keep_a,), odd_v)
        got_v = swap(odd_v, 1)
        back_a = swap_rep(send_a, 1)
        lists = [(even_l, got_l, rows_l), (even_v, got_v, rows_v)]
        cut_l = (rows_l + rows_v) // 32 * 16
        send_x, send_y = combine(
            order,
            (keep_a,),
            [diagonal(even_l, got_l, 0, cut_l)],
            [diagonal(even_l, got_l, cut_l, rows_l - cut_l), diagonal(even_v, got_v, 0, rows_v)],
        )
        from_x, from_y = swap(send_x, 2), swap(send_y, 4)
        keep_a, keep_u = combine(
            order,
            (send_x,),
            [(half_a, (keep_a, None, 0), (back_a, None, 0))],
            [(half_u + half_o, (keep_u, None, 0), (back_u, None, 0))],
        )
        back_a = swap_rep(keep_a, 2)
        to_x, to_y = combine(order, (keep_a,), *relay(lists, from_x, from_y, cut_l))
        last_x, last_y = swap(to_x, 2), swap(to_y, 4)
        keep_u, low = gate((to_x,), keep_u, low)
        back_u, low_other = swap_rep(keep_u, 1), swap_rep(low, 1)
        sum_l, keep_a = combine(
            order,
            (keep_u,),
            [
                total(even_l, got_l, last_x, last_y, 0, 0, rows_l),
                total(even_v, got_v, last_x, last_y, 0, rows_l, rows_v),
            ],
            [(half_a, (keep_a, None, 0), (back_a, None, 0))],
        )
        back_l, back_a = swap_rep(sum_l, 1), swap_rep(keep_a, 1)
        (sum_l,) = combine(order, (), [(rows_l + rows_v, (sum_l, None, 0), (back_l, None, 0))])
        back_l = swap_rep(sum_l, 2)
        grad_expand, grad_reduce, grad_output, *early = owner_parts(
            order, (sum_l,), width, hidden, keep_u, back_u, low, low_other
        )
        grad_triple, *late = triple_owner(order, (grad_expand,), width, keep_a, back_a, sum_l, back_l)
    else:
        def natural(even, odd):
            return [(odd if at % 2 else even)[at // 2] for at in range(PARTS)]

        parts = [natural(*one) for one in (
            (even_u, odd_u), (even_o, odd_o), (even_d, odd_d), (even_a, odd_a), (even_l, odd_l), (even_v, odd_v)
        )]
        found = []
        for up, out, down, first, last, late in zip(*parts):
            last = jnp.concatenate([last, late])
            halves = [
                jnp.concatenate([up[at * (rows_u // 2) : (at + 1) * (rows_u // 2)], out[at * (rows_o // 2) : (at + 1) * (rows_o // 2)]])
                for at in range(2)
            ]
            one = owner_parts(order, (), width, hidden, *halves, down[: rows_d // 2], down[rows_d // 2 :])
            found.append((*one, *triple_owner(order, (), width, *jnp.split(first, 2), last, jnp.zeros_like(last))))
        grad_expand, grad_reduce, grad_output, *early, grad_triple, g_1, s_1, q_1, v_1 = [list(one) for one in zip(*found)]
        late = [g_1, s_1, q_1, v_1]
        grad_expand, grad_reduce, grad_output, grad_triple = [
            scatter(jnp.concatenate(one).astype(BF)).astype(F32)
            for one in (grad_expand, grad_reduce, grad_output, grad_triple)
        ]

    def one_vector(*rows):
        if local:
            return jnp.concatenate([one.reshape(-1) for one in rows]) if len(rows) > 1 else rows[0].reshape(-1)
        whole = jnp.concatenate([one.reshape(-1) for parts in zip(*rows) for one in parts])
        return scatter(whole.astype(BF)).astype(F32)

    return (
        out_tokens,
        grad_tokens,
        one_vector(late[0]),
        one_vector(late[1]),
        grad_triple,
        one_vector(late[2], late[3]),
        grad_output,
        one_vector(early[2]),
        one_vector(early[0]),
        one_vector(early[1]),
        grad_expand,
        one_vector(early[4]),
        grad_reduce,
        one_vector(early[3]),
    )


def solution(mesh):
    return jax.shard_map(
        functools.partial(shards, mesh.shape["shard"]),
        mesh=mesh,
        in_specs=(
            P(("shard", "rep"), None),
            P(("shard", "rep")),
            P(("shard", "rep"), None),
            P("shard"),
            P("shard"),
            P("shard", None),
            P("shard"),
            P("shard", None),
            P("shard"),
            P("shard"),
            P("shard"),
            P("shard", None),
            P("shard"),
            P("shard", None),
            P("shard"),
        ),
        out_specs=(
            P(("shard", "rep"), None),
            P(("shard", "rep"), None),
            P("shard"),
            P("shard"),
            P("shard", None),
            P("shard"),
            P("shard", None),
            P("shard"),
            P("shard"),
            P("shard"),
            P("shard", None),
            P("shard"),
            P("shard", None),
            P("shard"),
        ),
        check_vma=False,
    )
```

```python
import functools

import jax
import jax.numpy as jnp
from jax import lax
from jax.experimental import pallas as pl
from jax.experimental.pallas import tpu as pltpu
from jax.sharding import PartitionSpec as P

HEAD_DIM = 64
PARTS = 8
HALVES = 3
GAIN_ONE, SHIFT_ONE, BIAS_OUT, GAIN_TWO, SHIFT_TWO, BIAS_DOWN, BIAS_QV = range(7)
VECTOR_ROWS = ((0,), (1,), (2,), (3,), (4,), (5,), (6, 7))
EPSILON = 1e-05
BF = jnp.bfloat16
F32 = jnp.float32
NEVER = -1e30
ROOT = 0.7978845608028654
MIB = 1 << 20
VMEM = 60


def dot_nn(left, right):
    return lax.dot_general(left, right, (((1,), (0,)), ((), ())), preferred_element_type=F32)


def dot_nt(left, right):
    return lax.dot_general(left, right, (((1,), (1,)), ((), ())), preferred_element_type=F32)


def dot_tn(left, right):
    return lax.dot_general(left, right, (((0,), (0,)), ((), ())), preferred_element_type=F32)


def normalise(values):
    center = values - jnp.mean(values, axis=-1, keepdims=True)
    variance = jnp.mean(center * center, axis=-1, keepdims=True)
    scale = lax.rsqrt(variance + EPSILON)
    return center * scale, scale


def norm_back(values, incoming, gain):
    unit, scale = normalise(values)
    scaled = incoming * gain
    first = jnp.mean(scaled, axis=-1, keepdims=True)
    second = jnp.mean(scaled * unit, axis=-1, keepdims=True)
    back = scale * (scaled - first - unit * second)
    return back, jnp.sum(incoming * unit, axis=0, keepdims=True)


def whole_spec(shape):
    return pl.BlockSpec(shape, lambda *_: (0,) * len(shape))


def once_spec(shape):
    return pl.BlockSpec(shape, lambda *_: (0,) * len(shape), pipeline_mode=pl.Buffered(1))


def cost(flops, moved, exps=0):
    return pl.CostEstimate(flops=int(flops), bytes_accessed=int(moved), transcendentals=int(exps))


def run(
    kernel, name, order, deps, inputs, in_specs, out_specs, out_shape, scratch=(), grid=(1,), estimate=None, vmem=VMEM
):
    count = len(deps)

    def body(order_ref, *refs):
        kernel(order_ref, *refs[count:])

    return pl.pallas_call(
        body,
        grid_spec=pltpu.PrefetchScalarGridSpec(
            num_scalar_prefetch=1,
            grid=grid,
            in_specs=[pl.BlockSpec(memory_space=pl.ANY)] * count + list(in_specs),
            out_specs=out_specs,
            scratch_shapes=list(scratch),
        ),
        out_shape=out_shape,
        compiler_params=pltpu.CompilerParams(vmem_limit_bytes=vmem * MIB),
        cost_estimate=estimate,
        name=name,
    )(order, *deps, *inputs)


def gate(deps, *values):
    count, size = len(deps), len(values)
    return pl.pallas_call(
        lambda *_: None,
        in_specs=[pl.BlockSpec(memory_space=pl.ANY)] * (count + size),
        out_specs=[pl.BlockSpec(memory_space=pl.ANY)] * size,
        out_shape=[jax.ShapeDtypeStruct(one.shape, one.dtype) for one in values],
        input_output_aliases={count + at: at for at in range(size)},
        name="gate",
    )(*deps, *values)


def fill_weight(order_ref, pieces, first, blocks, out_ref, rows, lead=None):
    mine = order_ref[0]
    for piece in range(PARTS):
        place = pl.ds(pl.multiple_of((piece ^ mine) * rows, 32), rows)
        for at in range(blocks):
            tile = piece_rows(pieces, piece, first + at * rows, rows)
            if lead is None:
                out_ref[place, at * 128 : (at + 1) * 128] = tile
            else:
                group, inside = divmod(at, lead)
                out_ref[group, place, inside * 128 : (inside + 1) * 128] = tile


def piece_rows(pieces, piece, start, rows):
    if len(pieces) == PARTS or piece < 6:
        return pieces[piece][start : start + rows, :]
    cut = pieces[6].shape[0]
    if start < cut:
        return pieces[2 * piece - 6][start : start + rows, :]
    return pieces[2 * piece - 5][start - cut : start - cut + rows, :]


def put_pieces(order_ref, even_ref, odd_ref, place, value):
    chip = lax.shift_right_logical(order_ref[0], 1)
    for core in range(2):
        @pl.when(lax.rem(order_ref[0], 2) == core)
        def _():
            for part in range(PARTS):
                out_ref = even_ref if part % 2 == core else odd_ref
                out_ref[(part // 2) ^ chip, place, :] = value(part)


def project_kernel(width, count, order_ref, *refs):
    pieces, (x_ref, qkv_ref, turned_ref, vector_ref, up_ref, w_ref, v_ref) = refs[:count], refs[count:]
    share = width // PARTS

    @pl.when(pl.program_id(0) == 0)
    def _():
        fill_weight(order_ref, pieces, 0, 3 * width // 128, w_ref, share, width // 128)
        for piece in range(PARTS):
            v_ref[piece ^ order_ref[0]] = piece_rows(pieces, piece, 3 * width // 128 * share, 16).astype(F32)
        vector_ref[...] = jnp.zeros_like(vector_ref)
        for out, places in enumerate(VECTOR_ROWS):
            parts = [
                v_ref[at // len(places), places[at % len(places)] : places[at % len(places)] + 1, :share]
                for at in range(PARTS * len(places))
            ]
            for at in range(len(places)):
                row = jnp.concatenate(parts[at * PARTS : (at + 1) * PARTS], axis=1)
                vector_ref[out + at : out + at + 1, :] = row
        wide = up_ref.shape[1] // PARTS // 128
        for part in range(PARTS):
            for at in range(wide):
                first = (part * wide + at) * 128
                up_ref[:, first : first + 128] = v_ref[part, 8 + at : 9 + at, :]

    unit, _ = normalise(x_ref[...].astype(F32))
    normed = (unit * vector_ref[GAIN_ONE : GAIN_ONE + 1, :] + vector_ref[SHIFT_ONE : SHIFT_ONE + 1, :]).astype(BF)
    turned_ref[...] = normed.T
    for at in range(3):
        product = dot_nn(normed, w_ref[at])
        if at != 1:
            product = product + vector_ref[BIAS_QV + at // 2 : BIAS_QV + at // 2 + 1, :]
        qkv_ref[at] = product.astype(BF)


def project(order, deps, pack, x, hidden):
    rows, width = x.shape
    block = min(256, rows)
    return run(
        functools.partial(project_kernel, width, len(pack)),
        "project",
        order,
        deps,
        (*pack, x),
        [whole_spec(one.shape) for one in pack] + [pl.BlockSpec((block, width), lambda i, *_: (i, 0))],
        [
            pl.BlockSpec((3, block, width), lambda i, *_: (0, i, 0)),
            pl.BlockSpec((width, block), lambda i, *_: (0, i)),
            whole_spec((8, width)),
            whole_spec((1, hidden)),
        ],
        [
            jax.ShapeDtypeStruct((3, rows, width), BF),
            jax.ShapeDtypeStruct((width, rows), BF),
            jax.ShapeDtypeStruct((8, width), F32),
            jax.ShapeDtypeStruct((1, hidden), F32),
        ],
        [pltpu.VMEM((3, width, width), BF), pltpu.VMEM((PARTS, 16, 128), F32)],
        (rows // block,),
        cost(6 * rows * width * width, 14 * rows * width),
    )


def attend_forward_kernel(block, order_ref, col_ref, row_ref, qkv_ref, mixed_ref, log_ref, bias_ref):
    rows = row_ref.shape[1]

    @pl.when(pl.program_id(0) == 0)
    def _():
        for first in range(0, rows, block):
            at = lax.broadcasted_iota(jnp.int32, (block, rows), 0) + first
            key = lax.broadcasted_iota(jnp.int32, (block, rows), 1)
            same = col_ref[first : first + block, :] == row_ref[...]
            bias_ref[first : first + block, :] = jnp.where(same & (key <= at), 0.0, NEVER)

    lane = lax.broadcasted_iota(jnp.int32, (block, 128), 1)
    for first in range(0, rows, block):
        last = first + block
        queries = qkv_ref[0, first:last, :] * jnp.asarray(0.125, BF)
        outs, logs = [], []
        for head in range(2):
            mine = (lane < HEAD_DIM) if head == 0 else (lane >= HEAD_DIM)
            scores = dot_nt(jnp.where(mine, queries, jnp.zeros_like(queries)), qkv_ref[1, :last, :])
            scores = scores + bias_ref[first:last, :last]
            largest = jnp.max(scores, axis=-1, keepdims=True)
            expo = jnp.exp(scores - largest)
            total = jnp.sum(expo, axis=-1, keepdims=True)
            outs.append(dot_nn(expo.astype(BF), qkv_ref[2, :last, :]) / total)
            logs.append(largest + jnp.log(total))
        mixed_ref[first:last, :] = jnp.where(lane < HEAD_DIM, outs[0], outs[1]).astype(BF)
        log_ref[0, first:last, :] = jnp.where(lane < HEAD_DIM, logs[1], logs[0])


def attend_forward(order, deps, col, row, qkv, half):
    _, rows, width = qkv.shape
    pairs = width // 128 // HALVES
    block = min(256, rows)
    return run(
        functools.partial(attend_forward_kernel, block),
        "attend_forward",
        order,
        deps,
        (col, row, qkv),
        [
            whole_spec(col.shape),
            whole_spec(row.shape),
            pl.BlockSpec((3, rows, 128), lambda i, *_: (0, 0, i + half * pairs)),
        ],
        [
            pl.BlockSpec((rows, 128), lambda i, *_: (0, i)),
            pl.BlockSpec((1, rows, 128), lambda i, *_: (i, 0, 0)),
        ],
        [
            jax.ShapeDtypeStruct((rows, width // HALVES), BF),
            jax.ShapeDtypeStruct((pairs, rows, 128), F32),
        ],
        [pltpu.VMEM((rows, rows), F32)],
        (pairs,),
        cost(8 * rows * rows * width, 6 * rows * width, rows * rows * pairs),
    )


def split_lanes(value, lane):
    high = value.astype(BF)
    rest = value - high.astype(F32)
    middle = rest.astype(BF)
    low = (rest - middle.astype(F32)).astype(BF)
    inside = lax.rem(lane, HEAD_DIM)
    zero = jnp.zeros_like(high)
    return jnp.where(inside == 0, high, jnp.where(inside == 1, middle, jnp.where(inside == 2, low, zero)))


def attend_backward_kernel(
    block, order_ref, col_ref, row_ref, qkv_ref, mixed_ref, log_ref, grad_ref, out_ref, bias_ref, q_ref, k_ref, d_ref, v_ref,
    dq_ref,
):
    rows = row_ref.shape[1]

    @pl.when(pl.program_id(0) == 0)
    def _():
        for first in range(0, rows, block):
            key = lax.broadcasted_iota(jnp.int32, (block, rows), 0) + first
            at = lax.broadcasted_iota(jnp.int32, (block, rows), 1)
            same = col_ref[first : first + block, :] == row_ref[...]
            bias_ref[first : first + block, :] = jnp.where(same & (key <= at), 0.0, NEVER)

    lane = lax.broadcasted_iota(jnp.int32, (block, 128), 1)
    below = lane < HEAD_DIM
    minus = jnp.where(lax.rem(lane, HEAD_DIM) < 3, -1.0, 0.0).astype(BF)
    for first in range(0, rows, block):
        last = first + block
        queries = qkv_ref[0, first:last, :] * jnp.asarray(0.125, BF)
        keys = qkv_ref[1, first:last, :]
        values = qkv_ref[2, first:last, :]
        grads = grad_ref[first:last, :]
        product = grads.astype(F32) * mixed_ref[first:last, :].astype(F32)
        sums = [
            jnp.sum(jnp.where(below, product, 0.0), axis=-1, keepdims=True),
            jnp.sum(jnp.where(below, 0.0, product), axis=-1, keepdims=True),
        ]
        logs = split_lanes(log_ref[0, first:last, :], lane)
        inner = split_lanes(jnp.where(below, sums[1], sums[0]), lane)
        for head in range(2):
            mine = below if head == 0 else lane >= HEAD_DIM
            q_ref[head, first:last, :] = jnp.where(mine, queries, logs)
            k_ref[head, first:last, :] = jnp.where(mine, keys, minus)
            d_ref[head, first:last, :] = jnp.where(mine, grads, inner)
            v_ref[head, first:last, :] = jnp.where(mine, values, minus)

    for first in range(0, rows, block):
        last = first + block
        key_parts, value_parts, query_parts = [], [], []
        for head in range(2):
            scores = dot_nt(k_ref[head, first:last, :], q_ref[head, first:, :]) + bias_ref[first:last, first:]
            probs = jnp.exp(scores)
            slopes = probs * dot_nt(v_ref[head, first:last, :], d_ref[head, first:, :])
            slopes = slopes.astype(BF)
            value_parts.append(dot_nn(probs.astype(BF), d_ref[head, first:, :]))
            key_parts.append(dot_nn(slopes, q_ref[head, first:, :]))
            query_parts.append(dot_tn(slopes, k_ref[head, first:last, :]))
        out_ref[1, first:last, :] = jnp.where(below, key_parts[0], key_parts[1]).astype(BF)
        out_ref[2, first:last, :] = jnp.where(below, value_parts[0], value_parts[1]).astype(BF)
        side = lax.broadcasted_iota(jnp.int32, (rows - first, 128), 1) < HEAD_DIM
        part = jnp.where(side, query_parts[0], query_parts[1])
        if first == 0:
            dq_ref[...] = part
        else:
            dq_ref[first:, :] += part
    out_ref[0] = (dq_ref[...] * 0.125).astype(BF)


def attend_backward(order, deps, col, row, qkv, mixed, log_total, grad, half):
    _, rows, width = qkv.shape
    pairs = width // 128 // HALVES
    block = min(256, rows)
    return run(
        functools.partial(attend_backward_kernel, block),
        "attend_backward",
        order,
        deps,
        (col, row, qkv, mixed, log_total, grad),
        [
            whole_spec(col.shape),
            whole_spec(row.shape),
            pl.BlockSpec((3, rows, 128), lambda i, *_: (0, 0, i + half * pairs)),
            pl.BlockSpec((rows, 128), lambda i, *_: (0, i)),
            pl.BlockSpec((1, rows, 128), lambda i, *_: (i, 0, 0)),
            pl.BlockSpec((rows, 128), lambda i, *_: (0, i + half * pairs)),
        ],
        pl.BlockSpec((3, rows, 128), lambda i, *_: (0, 0, i)),
        jax.ShapeDtypeStruct((3, rows, width // HALVES), BF),
        [pltpu.VMEM((rows, rows), F32)] + [pltpu.VMEM((2, rows, 128), BF)] * 4 + [pltpu.VMEM((rows, 128), F32)],
        (pairs,),
        cost(20 * rows * rows * width, 10 * rows * width, rows * rows * pairs),
    )


def middle_kernel(width, hidden, steps, count, order_ref, *refs):
    pieces, refs = refs[:count], refs[count:]
    x_ref, seg_ref, cot_ref, vector_ref, bias_ref, *refs = refs
    mixed_refs, refs = refs[:HALVES], refs[HALVES:]
    turned_ref, feed_ref, h_ref, e_ref, out_ref, grad_ref, branch_ref, mixed_grad_ref, sums_ref, wide_ref, *refs = refs
    wo_ref, we_ref, wr_ref = refs
    share = width // PARTS

    @pl.when(pl.program_id(0) == 0)
    def _():
        fill_weight(order_ref, pieces, 0, width // 128, wo_ref, share)
        fill_weight(order_ref, pieces, width // 128 * share, hidden // 128, we_ref, share)
        fill_weight(order_ref, pieces, (width + hidden) // 128 * share, width // 128, wr_ref, hidden // PARTS)
        sums_ref[...] = jnp.zeros_like(sums_ref)
        wide_ref[...] = jnp.zeros_like(wide_ref)

    def vector(at):
        return vector_ref[at : at + 1, :]

    mixed = jnp.concatenate([one[...] for one in mixed_refs], axis=1)
    middle = x_ref[...].astype(F32) + dot_nn(mixed, wo_ref[...]) + vector(BIAS_OUT)
    unit, scale = normalise(middle)
    normed = (unit * vector(GAIN_TWO) + vector(SHIFT_TWO)).astype(BF)
    turned_ref[...] = normed.T
    live = seg_ref[...] >= 0
    feed = jnp.where(live, cot_ref[...].astype(F32), 0.0)
    feed_low = feed.astype(BF)
    feed_ref[...] = feed_low
    for at in range(0, hidden, 256):
        cols = slice(at, at + 256)
        u = dot_nn(normed, we_ref[:, cols]) + bias_ref[:, cols]
        hidden_grad = dot_nt(feed_low, wr_ref[cols, :])
        square = u * u
        tanh = jnp.tanh(u * (ROOT + (ROOT * 0.044715) * square))
        half = 0.5 + 0.5 * tanh
        h_ref[:, cols] = (u * half).astype(BF)
        slope = half + u * (0.5 - 0.5 * (tanh * tanh)) * (ROOT + (3 * 0.044715 * ROOT) * square)
        e_part = (hidden_grad * slope).astype(BF)
        e_ref[:, cols] = e_part
        wide_ref[:, cols] += jnp.sum(e_part.astype(F32), axis=0, keepdims=True)
    total = middle + dot_nn(h_ref[...], wr_ref[...]) + vector(BIAS_DOWN)
    out_ref[...] = jnp.where(live, total, 0.0).astype(BF)
    back = dot_nt(e_ref[...], we_ref[...])
    scaled = back * vector(GAIN_TWO)
    mean = jnp.mean(scaled, axis=-1, keepdims=True)
    second = jnp.mean(scaled * unit, axis=-1, keepdims=True)
    grad = feed + scale * (scaled - mean - unit * second)
    grad_ref[...] = grad
    branch = grad.astype(BF)
    branch_ref[...] = branch
    mixed_grad_ref[...] = dot_nt(branch, wo_ref[...]).astype(BF)
    sums_ref[0:1, :] += jnp.sum(back * unit, axis=0, keepdims=True)
    sums_ref[1:2, :] += jnp.sum(back, axis=0, keepdims=True)
    sums_ref[2:3, :] += jnp.sum(branch.astype(F32), axis=0, keepdims=True)
    sums_ref[3:4, :] += jnp.sum(feed, axis=0, keepdims=True)


def make_middle(order, deps, pack, x, mixed, col, cot, vectors, bias):
    rows, width = x.shape
    hidden = bias.shape[1]
    block = min(256, rows)
    by_rows = pl.BlockSpec((block, width), lambda i, *_: (i, 0))
    by_wide = pl.BlockSpec((block, hidden), lambda i, *_: (i, 0))
    low = jax.ShapeDtypeStruct((rows, width), BF)
    return run(
        functools.partial(middle_kernel, width, hidden, rows // block, len(pack)),
        "middle",
        order,
        deps,
        (*pack, x, col, cot, vectors, bias, *mixed),
        [once_spec(one.shape) for one in pack]
        + [by_rows, pl.BlockSpec((block, 1), lambda i, *_: (i, 0)), by_rows]
        + [whole_spec(vectors.shape), whole_spec(bias.shape)]
        + [pl.BlockSpec((block, width // HALVES), lambda i, *_: (i, 0))] * HALVES,
        [pl.BlockSpec((width, block), lambda i, *_: (0, i)), by_rows, by_wide, by_wide]
        + [by_rows] * 4
        + [whole_spec((8, width)), whole_spec((1, hidden))],
        [
            jax.ShapeDtypeStruct((width, rows), BF),
            low,
            jax.ShapeDtypeStruct((rows, hidden), BF),
            jax.ShapeDtypeStruct((rows, hidden), BF),
            low,
            jax.ShapeDtypeStruct((rows, width), F32),
            low,
            low,
            jax.ShapeDtypeStruct((8, width), F32),
            jax.ShapeDtypeStruct((1, hidden), F32),
        ],
        [pltpu.VMEM((width, width), BF), pltpu.VMEM((width, hidden), BF), pltpu.VMEM((hidden, width), BF)],
        (rows // block,),
        cost(4 * rows * width * (width + 2 * hidden), 50 * rows * width, rows * hidden),
    )


def down_kernel(order_ref, h_ref, feed_ref, even_ref, odd_ref):
    grad = dot_tn(h_ref[...], feed_ref[...]).astype(BF)
    half, width = grad.shape[0] // 2, grad.shape[1]
    for core in range(2):
        @pl.when(lax.rem(order_ref[0], 2) == core)
        def _():
            for side in range(2):
                out_ref = even_ref if side == core else odd_ref
                for lane in range(width // 128):
                    out_ref[0, lane * half : (lane + 1) * half, :] = grad[
                        side * half : (side + 1) * half, lane * 128 : (lane + 1) * 128
                    ]


def down_grad(order, deps, h, feed):
    rows, hidden = h.shape
    width = feed.shape[1]
    pairs = PARTS // 2
    own = jax.ShapeDtypeStruct((pairs, hidden // PARTS * width // 128, 128), BF)
    own_spec = pl.BlockSpec((1, *own.shape[1:]), lambda i, order: (i ^ lax.shift_right_logical(order[0], 1), 0, 0))
    return run(
        down_kernel,
        "down_grad",
        order,
        deps,
        (h, feed),
        [pl.BlockSpec((rows, hidden // pairs), lambda i, *_: (0, i)), whole_spec(feed.shape)],
        [own_spec, own_spec],
        [own, own],
        (),
        (pairs,),
        cost(2 * rows * width * hidden, 4 * rows * hidden),
    )


def up_kernel(steps, order_ref, *refs):
    turned_ref, e_ref, branch_ref, sums_ref, wide_ref, *refs = refs
    mixed_refs, (even_ref, odd_ref, own_even_ref, own_odd_ref, t_ref) = refs[:HALVES], refs[HALVES:]
    step = pl.program_id(0)

    @pl.when(step < steps)
    def _():
        put_triple(order_ref, turned_ref[...], e_ref[...], even_ref, odd_ref, 0, False)

    @pl.when(step == steps)
    def _():
        width = branch_ref.shape[1]
        share, half = width // PARTS, width // 256
        mixed = jnp.concatenate([one[...] for one in mixed_refs], axis=1)
        t_ref[...] = dot_tn(mixed, branch_ref[...]).astype(BF)
        for lane in range(width // 128):
            base = lane * share + lane // half * 16
            put_pieces(
                order_ref, own_even_ref, own_odd_ref, slice(base, base + share),
                lambda part: t_ref[part * share : (part + 1) * share, lane * 128 : (lane + 1) * 128],
            )
        put_vectors(
            order_ref, own_even_ref, own_odd_ref, half * share, sums_ref,
            lambda part: [(at, part) for at in range(4)], wide_ref,
        )
        for one in (own_even_ref, own_odd_ref):
            one[:, 2 * half * share + 16 :, :] = jnp.zeros((PARTS // 2, 16, 128), BF)


def up_grad(order, deps, turned, e, branch, sums, wide, mixed):
    width, rows = turned.shape
    hidden = e.shape[1]
    steps = PARTS // 2
    share = width // PARTS
    part_rows = hidden // steps // 128 * share
    up = jax.ShapeDtypeStruct((PARTS // 2, hidden // 128 * share, 128), BF)
    own = jax.ShapeDtypeStruct((PARTS // 2, width // 128 * share + 32, 128), BF)
    up_spec = pl.BlockSpec((PARTS // 2, part_rows, 128), lambda i, *_: (0, jnp.minimum(i, steps - 1), 0))
    return run(
        functools.partial(up_kernel, steps),
        "up_grad",
        order,
        deps,
        (turned, e, branch, sums, wide, *mixed),
        [whole_spec(turned.shape), pl.BlockSpec((rows, hidden // steps), lambda i, *_: (0, jnp.minimum(i, steps - 1)))]
        + [whole_spec(one.shape) for one in (branch, sums, wide, *mixed)],
        [up_spec, up_spec, whole_spec(own.shape), whole_spec(own.shape)],
        [up, up, own, own],
        [pltpu.VMEM((width, width), BF)],
        (steps + 1,),
        cost(2 * rows * width * (hidden + width), 4 * rows * hidden),
    )


def put_vectors(order_ref, even_ref, odd_ref, base, sums_ref, shares, wide_ref=None):
    share = sums_ref.shape[1] // PARTS
    sums = sums_ref[...]
    blank = jnp.zeros((1, 128 - share), F32)

    def value(part):
        rows = [
            jnp.concatenate([sums[row : row + 1, at * share : (at + 1) * share], blank], axis=1)
            for row, at in shares(part)
        ]
        if wide_ref is not None:
            size = wide_ref.shape[1] // PARTS
            rows += [wide_ref[:, at : at + 128] for at in range(part * size, (part + 1) * size, 128)]
        rows.append(jnp.zeros((16 - len(rows), 128), F32))
        return jnp.concatenate(rows, axis=0).astype(BF)

    put_pieces(order_ref, even_ref, odd_ref, slice(base, base + 16), value)


def put_triple(order_ref, turned, grads, even_ref, odd_ref, base, summed=True):
    share = turned.shape[0] // PARTS
    product = dot_nn(turned, grads).astype(BF)
    for lane in range(grads.shape[1] // 128):
        put_pieces(
            order_ref, even_ref, odd_ref, pl.ds(base + lane * share, share),
            lambda part: product[part * share : (part + 1) * share, lane * 128 : (lane + 1) * 128],
        )
    return jnp.sum(grads.astype(F32), axis=0, keepdims=True) if summed else None


def triple_kernel(count, order_ref, turned_ref, *refs):
    grads, (even_ref, odd_ref, sum_ref) = refs[:count], refs[count:]
    whole = jnp.concatenate([one[0] for one in grads], axis=1)
    sum_ref[0] = put_triple(order_ref, turned_ref[...], whole, even_ref, odd_ref, 0)


def triple_grad(order, deps, turned, *grads):
    width, rows = turned.shape
    third, count = grads[0].shape[2], len(grads)
    part_rows = count * third // 128 * width // PARTS
    own = jax.ShapeDtypeStruct((PARTS // 2, 3 * part_rows, 128), BF)
    own_spec = pl.BlockSpec((PARTS // 2, part_rows, 128), lambda i, *_: (0, i, 0))
    by_third = pl.BlockSpec((1, rows, third), lambda i, *_: (i, 0, 0))
    return run(
        functools.partial(triple_kernel, count),
        "triple_grad",
        order,
        deps,
        (turned, *grads),
        [once_spec(turned.shape)] + [by_third] * count,
        [own_spec, own_spec, pl.BlockSpec((1, 1, count * third), lambda i, *_: (i, 0, 0))],
        [own, own, jax.ShapeDtypeStruct((3, 1, count * third), F32)],
        (),
        (3,),
        cost(6 * rows * width * third * count, 8 * rows * width),
    )


def input_kernel(width, steps, count, order_ref, *refs):
    pieces, refs = refs[:count], refs[count:]
    x_ref, *refs = refs
    third_refs, refs = refs[:HALVES], refs[HALVES:]
    middle_ref, vector_ref, sum_ref, late_ref, even_ref, odd_ref, out_ref, w_ref, sums_ref = refs
    step = pl.program_id(0)
    share, third = width // PARTS, width // HALVES

    @pl.when(step == 0)
    def _():
        fill_weight(order_ref, pieces, 0, 3 * width // 128, w_ref, share, width // 128)
        sums_ref[...] = jnp.zeros_like(sums_ref)

    back = None
    for at in range(3):
        one = dot_nt(jnp.concatenate([ref[at] for ref in third_refs], axis=1), w_ref[at])
        back = one if back is None else back + one
    part, gain_sum = norm_back(x_ref[...].astype(F32), back, vector_ref[GAIN_ONE : GAIN_ONE + 1, :])
    out_ref[...] = (middle_ref[...] + part).astype(BF)
    sums_ref[0:1, :] += gain_sum
    sums_ref[1:2, :] += jnp.sum(back, axis=0, keepdims=True)

    @pl.when(step == steps - 1)
    def _():
        for row, at in ((2, 0), (3, 2)):
            sums_ref[row : row + 1, : 2 * third] = sum_ref[at]
            sums_ref[row : row + 1, 2 * third :] = late_ref[at]
        put_vectors(
            order_ref, even_ref, odd_ref, 0, sums_ref,
            lambda part: [(0, part), (1, part)]
            + [(2 + at // PARTS, at % PARTS) for at in (2 * part, 2 * part + 1)],
        )


def input_grad(order, deps, pack, x, grads, middle_grad, vectors, sums, late):
    rows, width = x.shape
    third = width // HALVES
    block = min(512, rows)
    steps = rows // block
    own = jax.ShapeDtypeStruct((PARTS // 2, 16, 128), BF)
    by_rows = pl.BlockSpec((block, width), lambda i, *_: (i, 0))
    by_third = pl.BlockSpec((3, block, third), lambda i, *_: (0, i, 0))
    return run(
        functools.partial(input_kernel, width, steps, len(pack)),
        "input_grad",
        order,
        deps,
        (*pack, x, *grads, middle_grad, vectors, sums, late),
        [once_spec(one.shape) for one in pack]
        + [by_rows]
        + [by_third] * HALVES
        + [by_rows, whole_spec(vectors.shape), whole_spec(sums.shape), whole_spec(late.shape)],
        [whole_spec(own.shape), whole_spec(own.shape), by_rows],
        [own, own, jax.ShapeDtypeStruct((rows, width), BF)],
        [pltpu.VMEM((3, width, width), BF), pltpu.VMEM((8, width), F32)],
        (steps,),
        cost(6 * rows * width * width, 24 * rows * width),
    )


def owner_kernel(width, hidden, order_ref, mine_ref, other_ref, low_ref, low_other_ref, *outs):
    expand_ref, reduce_ref, output_ref, *vector_refs = outs
    share, tall, half = width // PARTS, hidden // PARTS, width // 256
    ups = hidden // 256
    bit = order_ref[1] & 1
    for place in range(2):
        @pl.when(bit == place)
        def _():
            for side in range(2):
                up_ref, down_ref = (mine_ref, low_ref) if side == place else (other_ref, low_other_ref)
                for at in range(ups):
                    first = (side * ups + at) * 128
                    expand_ref[:, first : first + 128] = up_ref[at * share : (at + 1) * share, :].astype(F32)
                base = ups * share
                for at in range(half):
                    first = (side * half + at) * 128
                    output_ref[:, first : first + 128] = up_ref[
                        base + at * share : base + (at + 1) * share, :
                    ].astype(F32)
                    reduce_ref[:, first : first + 128] = down_ref[at * tall : (at + 1) * tall, :].astype(F32)
                if side == 0:
                    vectors = up_ref[base + half * share : base + half * share + 16, :].astype(F32)
                    for at in range(4):
                        vector_refs[at][...] = vectors[at : at + 1, :share]
                    vector_refs[4][...] = vectors[4 : 4 + tall // 128, :]


def owner_parts(order, deps, width, hidden, mine, other, low, low_other):
    share, tall = width // PARTS, hidden // PARTS
    shapes = [(share, hidden), (tall, width), (share, width)] + [(1, share)] * 4 + [(tall // 128, 128)]
    return run(
        functools.partial(owner_kernel, width, hidden),
        "owner_parts",
        order,
        deps,
        (mine, other, low, low_other),
        [whole_spec(one.shape) for one in (mine, other, low, low_other)],
        [whole_spec(one) for one in shapes],
        [jax.ShapeDtypeStruct(one, F32) for one in shapes],
        (),
        (1,),
        cost(0, 6 * mine.size),
    )


def triple_owner_kernel(width, order_ref, mine_ref, other_ref, last_ref, more_ref, out_ref, *vector_refs):
    last = last_ref, more_ref
    share, tiles_each = width // PARTS, width // HALVES // 128
    tiles_half = 3 * tiles_each
    for place in range(2):
        @pl.when((order_ref[1] & 1) == place)
        def _():
            for index in range(2 * tiles_half):
                side, start = divmod(index, tiles_half)
                at, inside = divmod(index, 2 * tiles_each)
                column = (at * HALVES * tiles_each + inside) * 128
                ref = mine_ref if side == place else other_ref
                out_ref[:, column : column + 128] = ref[start * share : (start + 1) * share, :].astype(F32)
    for at in range(3):
        for tile in range(tiles_each):
            rows = slice((at * tiles_each + tile) * share, (at * tiles_each + tile + 1) * share)
            column = ((at * HALVES + 2) * tiles_each + tile) * 128
            out_ref[:, column : column + 128] = last[0][rows, :].astype(F32) + last[1][rows, :].astype(F32)
    rows = slice(3 * tiles_each * share, 3 * tiles_each * share + 16)
    vectors = last[0][rows, :].astype(F32) + last[1][rows, :].astype(F32)
    for at in range(4):
        vector_refs[at][...] = vectors[at : at + 1, :share]


def triple_owner(order, deps, width, *terms):
    shapes = [(width // PARTS, 3 * width)] + [(1, width // PARTS)] * 4
    return run(
        functools.partial(triple_owner_kernel, width),
        "triple_owner",
        order,
        deps,
        terms,
        [whole_spec(one.shape) for one in terms],
        [whole_spec(one) for one in shapes],
        [jax.ShapeDtypeStruct(one, F32) for one in shapes],
        (),
        (1,),
        cost(0, 12 * terms[0].size),
    )


def tiles(matrix):
    rows, cols = matrix.shape
    return matrix.reshape(rows, cols // 128, 128).transpose(1, 0, 2).reshape(-1, 128)


def untiles(packed, rows):
    return packed.reshape(-1, rows, 128).transpose(1, 0, 2).reshape(rows, -1)


def swap(value, mask):
    return lax.ppermute(value, "shard", [(at, at ^ mask) for at in range(PARTS)])


def swap_rep(value, mask):
    count = lax.axis_size("rep")
    return lax.ppermute(value, "rep", [(at, at ^ mask) for at in range(count)])


def combine_kernel(plan, order_ref, *refs):
    outs = refs[len(refs) - len(plan) :]
    for out_ref, segments in zip(outs, plan):
        at = 0
        for rows, terms in segments:
            total = None
            for source, start in terms:
                ref = refs[source]
                if isinstance(start, tuple):
                    base, half, flip = start
                    bit = order_ref[1] & 1
                    start = pl.multiple_of(base + (1 - bit if flip else bit) * half, 16)
                    rows_at = pl.ds(start, rows)
                else:
                    rows_at = slice(start, start + rows)
                one = ref[0, rows_at, :] if len(ref.shape) == 3 else ref[rows_at, :]
                if len(terms) > 1:
                    one = one.astype(F32)
                total = one if total is None else total + one
            out_ref[at : at + rows, :] = total.astype(BF)
            at += rows


def combine(order, deps, *outs):
    arrays, specs, places, plan, shapes = [], [], {}, [], []
    for segments in outs:
        steps = []
        for rows, *terms in segments:
            sources = []
            for array, index, start in terms:
                key = (id(array), index)
                if key not in places:
                    places[key] = len(arrays)
                    arrays.append(array)
                    if index is None:
                        specs.append(once_spec(array.shape))
                    else:
                        specs.append(pl.BlockSpec((1, *array.shape[1:]), lambda *_, index=index: (index, 0, 0),
                            pipeline_mode=pl.Buffered(1)))
                sources.append((places[key], start))
            steps.append((rows, tuple(sources)))
        plan.append(tuple(steps))
        shapes.append(jax.ShapeDtypeStruct((sum(rows for rows, _ in steps), 128), BF))
    moved = sum(2 * 128 * one.shape[-2] for one in arrays) + sum(256 * one.shape[0] for one in shapes)
    return run(
        functools.partial(combine_kernel, tuple(plan)),
        "combine",
        order,
        deps,
        arrays,
        specs,
        [whole_spec(one.shape) for one in shapes],
        shapes,
        (),
        (1,),
        cost(0, moved),
        24,
    )


def pack_kernel(plan, order_ref, *refs):
    outs = refs[len(refs) - len(plan) :]
    for out_ref, blocks in zip(outs, plan):
        at = 0
        for source, first, rows, column, columns in blocks:
            if rows == 1 and columns:
                if at % 16 == 0:
                    out_ref[at : at + 16, :] = jnp.zeros((16, 128), BF)
            out_ref[at : at + rows, :columns] = refs[source][first : first + rows, column : column + columns]
            at += rows


def pack_parts(order, deps, inputs, plan):
    shapes = [jax.ShapeDtypeStruct((-(-sum(one[2] for one in blocks) // 16) * 16, 128), BF) for blocks in plan]
    return run(
        functools.partial(pack_kernel, plan),
        "pack",
        order,
        deps,
        inputs,
        [whole_spec(one.shape) for one in inputs],
        [whole_spec(one.shape) for one in shapes],
        shapes,
        (),
        (1,),
        cost(0, sum(4 * one.size for one in inputs)),
    )


def pack_plans(share, width, hidden):
    triple = [(0, 0, share, 128 * at, 128) for at in range(3 * width // 128)]
    triple += [(at, 0, 1, 0, share) for at in range(1, 9)]
    triple += [(9, at, 1, 0, 128) for at in range(hidden // PARTS // 128)]
    others = [(0, 0, share, 128 * at, 128) for at in range(width // 128)]
    others += [(1, 0, share, 128 * at, 128) for at in range(hidden // 128)]
    others += [(2, 0, hidden // PARTS, 128 * at, 128) for at in range(width // 128)]
    return [triple], [others]


def vector_rows(share, small):
    *narrow, double, wide = small
    narrow += [double[:share], double[share:]]
    return [one.reshape(1, -1) for one in narrow] + [wide.reshape(-1, 128)]


def scatter(part):
    return lax.psum(lax.psum_scatter(part, "shard", scatter_dimension=0, tiled=True), "rep")


def diagonal(even, got, start, rows):
    return (rows, (even, 3, start), (got, 3, start))


def total(even, got, from_x, from_y, start, base, rows):
    return (rows, (even, 0, start), (got, 0, start), (from_x, None, base), (from_y, None, base))


def relay(lists, from_x, from_y, cut):
    outs = []
    for index, brought, upper in ((1, from_y, False), (2, from_x, True)):
        segments, first = [], 0
        for even, got, rows in lists:
            last = first + rows
            for start, stop in ((first, min(last, cut)), (max(first, cut), last)):
                if start >= stop:
                    continue
                terms = [(even, index, start - first), (got, index, start - first)]
                if (start < cut) == upper:
                    terms.append((brought, None, start if upper else start - cut))
                segments.append((stop - start, *terms))
            first = last
        outs.append(segments)
    return outs


def shards(
    count,
    tokens,
    segments,
    cotangent,
    attend_gain,
    attend_shift,
    triple_weight,
    triple_bias,
    output_weight,
    output_bias,
    feed_gain,
    feed_shift,
    expand_weight,
    expand_bias,
    reduce_weight,
    reduce_bias,
):
    rows, width = tokens.shape
    hidden = expand_weight.shape[1]
    share = width // PARTS
    small = (attend_gain, attend_shift, output_bias, feed_gain, feed_shift, reduce_bias, triple_bias, expand_bias)
    plan_a, plan_b = pack_plans(share, width, hidden)
    col = segments.reshape(rows, 1)
    row = segments.reshape(1, rows)
    local = count == PARTS and lax.axis_size("rep") == 4
    if local:
        order = jnp.stack([lax.axis_index("shard"), lax.axis_index("rep")]).astype(jnp.int32)
        (own_a,) = pack_parts(order, (), (triple_weight, *vector_rows(share, small)), plan_a)
        x_a, y_a, c_a = swap(own_a, 2), swap(own_a, 4), swap(own_a, 1)
        cut_a = 9 * share
        (own_b,) = pack_parts(order, (own_a, col), (output_weight, expand_weight, reduce_weight), plan_b)
        send_y, send_x = combine(
            order, (own_b, c_a), [(cut_a, (x_a, None, 0))], [(own_a.shape[0] - cut_a, (y_a, None, cut_a))]
        )
        u_a, l_a = swap(send_y, 4), swap(send_x, 2)
        pack_a = (own_a, c_a, x_a, swap(x_a, 1), y_a, swap(y_a, 1), u_a, l_a, swap(u_a, 1), swap(l_a, 1))
        (own_b,) = gate((send_y,), own_b)
        x_b, y_b = swap(own_b, 2), swap(own_b, 4)
    else:
        order = jnp.zeros((2,), jnp.int32)
        weights = (triple_weight, output_weight, expand_weight, reduce_weight, small)
        weights = jax.tree.map(lambda one: lax.all_gather(one, "shard", axis=0, tiled=True), weights)
        weights = jax.tree.map(lambda one: one.reshape(PARTS, -1, *one.shape[1:]), weights)
        pack_a, pack_b = [], []
        for part in range(PARTS):
            vectors = vector_rows(share, [one[part] for one in weights[4]])
            pack_a += pack_parts(order, (), (weights[0][part], *vectors), plan_a)
            pack_b += pack_parts(order, (), [one[part] for one in weights[1:4]], plan_b)
    qkv, turned_one, vectors, bias_up = project(order, (own_b,) if local else (), pack_a, tokens, hidden)
    mixed, logs = [None] * HALVES, [None] * HALVES
    mixed[0], logs[0] = attend_forward(order, (), col, row, qkv, 0)
    mixed[1], logs[1] = attend_forward(order, (mixed[0],), col, row, qkv, 1)
    deps = (mixed[1],)
    if local:
        cut_b = own_b.shape[0] // 2
        send_y, send_x = combine(
            order, deps, [(cut_b, (x_b, None, 0))], [(own_b.shape[0] - cut_b, (y_b, None, cut_b))]
        )
        u_b, l_b = swap(send_y, 4), swap(send_x, 2)
        x_b, y_b, own_b = gate((send_y,), x_b, y_b, own_b)
        c_b, c_x_b, c_y_b = swap(own_b, 1), swap(x_b, 1), swap(y_b, 1)
        deps = (x_b,)
    mixed[2], logs[2] = attend_forward(order, deps, col, row, qkv, 2)
    if local:
        u_b, l_b = gate((mixed[2],), u_b, l_b)
        pack_b = (own_b, c_b, x_b, c_x_b, y_b, c_y_b, u_b, l_b, swap(u_b, 1), swap(l_b, 1))
    turned_two, feed, h, e, out_tokens, middle_grad, branch, mixed_grad, sums, wide = make_middle(
        order, (), pack_b, tokens, mixed, col, cotangent, vectors, bias_up
    )
    even_d, odd_d = down_grad(order, (), h, feed)
    deps = (even_d,)
    if local:
        got_d = swap(odd_d, 1)
    even_u, odd_u, even_o, odd_o = up_grad(order, deps, turned_two, e, branch, sums, wide, mixed)
    deps = (even_u,)
    rows_d, rows_u, rows_o = even_d.shape[1], even_u.shape[1], even_o.shape[1]
    if local:
        got_u, got_o = swap(odd_u, 1), swap(odd_o, 1)
        cut_d = rows_d // 2
        send_x, send_y = combine(
            order, deps, [diagonal(even_d, got_d, 0, cut_d)], [diagonal(even_d, got_d, cut_d, rows_d - cut_d)]
        )
        from_x, from_y = swap(send_x, 2), swap(send_y, 4)
        deps = (send_x,)
    grads = [attend_backward(order, deps, col, row, qkv, mixed[0], logs[0], mixed_grad, 0)]
    deps = (grads[0],)
    if local:
        cut_u = (rows_u + rows_o) // 32 * 16
        to_x, to_y, send_x, send_y = combine(
            order,
            deps,
            *relay([(even_d, got_d, rows_d)], from_x, from_y, cut_d),
            [diagonal(even_u, got_u, 0, cut_u)],
            [diagonal(even_u, got_u, cut_u, rows_u - cut_u), diagonal(even_o, got_o, 0, rows_o)],
        )
        down_x, down_y = swap(to_x, 2), swap(to_y, 4)
        from_x, from_y = swap(send_x, 2), swap(send_y, 4)
        deps = (to_x,)
    grads.append(attend_backward(order, deps, col, row, qkv, mixed[1], logs[1], mixed_grad, 1))
    even_a, odd_a, sum_a = triple_grad(order, (), turned_one, *grads)
    deps = (even_a,)
    rows_a = even_a.shape[1]
    if local:
        got_a = swap(odd_a, 1)
        half = rows_d // 2
        keep_d, send_d, to_x, to_y = combine(
            order,
            deps,
            [total(even_d, got_d, down_x, down_y, (0, half, False), (0, half, False), half)],
            [total(even_d, got_d, down_x, down_y, (0, half, True), (0, half, True), half)],
            *relay([(even_u, got_u, rows_u), (even_o, got_o, rows_o)], from_x, from_y, cut_u),
        )
        up_x, up_y = swap(to_x, 2), swap(to_y, 4)
        back_d = swap_rep(send_d, 1)
        deps = (keep_d,)
    grads.append(attend_backward(order, deps, col, row, qkv, mixed[2], logs[2], mixed_grad, 2))
    deps = (grads[2],)
    if local:
        cut_a = rows_a // 2
        half_u, half_o = rows_u // 2, rows_o // 2
        keep_d, keep_u, send_u, send_x, send_y = combine(
            order,
            deps,
            [(half, (keep_d, None, 0), (back_d, None, 0))],
            [
                total(even_u, got_u, up_x, up_y, (0, half_u, False), (0, half_u, False), half_u),
                total(even_o, got_o, up_x, up_y, (0, half_o, False), (rows_u, half_o, False), half_o),
            ],
            [
                total(even_u, got_u, up_x, up_y, (0, half_u, True), (0, half_u, True), half_u),
                total(even_o, got_o, up_x, up_y, (0, half_o, True), (rows_u, half_o, True), half_o),
            ],
            [diagonal(even_a, got_a, 0, cut_a)],
            [diagonal(even_a, got_a, cut_a, rows_a - cut_a)],
        )
        from_x, from_y = swap(send_x, 2), swap(send_y, 4)
        back_d, back_u = swap_rep(keep_d, 2), swap_rep(send_u, 1)
        deps = (keep_d,)
    even_l, odd_l, late = triple_grad(order, deps, turned_one, grads[2])
    rows_l, rows_v = even_l.shape[1], 16
    deps = (even_l,)
    if local:
        keep_u, to_x, to_y = combine(
            order,
            deps,
            [(half_u + half_o, (keep_u, None, 0), (back_u, None, 0))],
            *relay([(even_a, got_a, rows_a)], from_x, from_y, cut_a),
        )
        far_x, far_y = swap(to_x, 2), swap(to_y, 4)
        back_u = swap_rep(keep_u, 2)
        deps = (to_x,)
        (odd_l,) = gate(deps, odd_l)
        got_l = swap(odd_l, 1)
    even_v, odd_v, grad_tokens = input_grad(
        order, deps, pack_a, tokens, grads, middle_grad, vectors, sum_a, late
    )
    if local:
        half_a = rows_a // 2
        keep_a, send_a, low = combine(
            order,
            (even_v,),
            [total(even_a, got_a, far_x, far_y, (0, half_a, False), (0, half_a, False), half_a)],
            [total(even_a, got_a, far_x, far_y, (0, half_a, True), (0, half_a, True), half_a)],
            [(half, (keep_d, None, 0), (back_d, None, 0))],
        )
        (odd_v,) = gate((keep_a,), odd_v)
        got_v = swap(odd_v, 1)
        back_a = swap_rep(send_a, 1)
        lists = [(even_l, got_l, rows_l), (even_v, got_v, rows_v)]
        cut_l = (rows_l + rows_v) // 32 * 16
        send_x, send_y = combine(
            order,
            (keep_a,),
            [diagonal(even_l, got_l, 0, cut_l)],
            [diagonal(even_l, got_l, cut_l, rows_l - cut_l), diagonal(even_v, got_v, 0, rows_v)],
        )
        from_x, from_y = swap(send_x, 2), swap(send_y, 4)
        keep_a, keep_u = combine(
            order,
            (send_x,),
            [(half_a, (keep_a, None, 0), (back_a, None, 0))],
            [(half_u + half_o, (keep_u, None, 0), (back_u, None, 0))],
        )
        back_a = swap_rep(keep_a, 2)
        to_x, to_y = combine(order, (keep_a,), *relay(lists, from_x, from_y, cut_l))
        last_x, last_y = swap(to_x, 2), swap(to_y, 4)
        keep_u, low = gate((to_x,), keep_u, low)
        back_u, low_other = swap_rep(keep_u, 1), swap_rep(low, 1)
        sum_l, keep_a = combine(
            order,
            (keep_u,),
            [
                total(even_l, got_l, last_x, last_y, 0, 0, rows_l),
                total(even_v, got_v, last_x, last_y, 0, rows_l, rows_v),
            ],
            [(half_a, (keep_a, None, 0), (back_a, None, 0))],
        )
        back_l, back_a = swap_rep(sum_l, 1), swap_rep(keep_a, 1)
        (sum_l,) = combine(order, (), [(rows_l + rows_v, (sum_l, None, 0), (back_l, None, 0))])
        back_l = swap_rep(sum_l, 2)
        grad_expand, grad_reduce, grad_output, *early = owner_parts(
            order, (sum_l,), width, hidden, keep_u, back_u, low, low_other
        )
        grad_triple, *late = triple_owner(order, (grad_expand,), width, keep_a, back_a, sum_l, back_l)
    else:
        def natural(even, odd):
            return [(odd if at % 2 else even)[at // 2] for at in range(PARTS)]

        parts = [natural(*one) for one in (
            (even_u, odd_u), (even_o, odd_o), (even_d, odd_d), (even_a, odd_a), (even_l, odd_l), (even_v, odd_v)
        )]
        found = []
        for up, out, down, first, last, late in zip(*parts):
            last = jnp.concatenate([last, late])
            halves = [
                jnp.concatenate([up[at * (rows_u // 2) : (at + 1) * (rows_u // 2)], out[at * (rows_o // 2) : (at + 1) * (rows_o // 2)]])
                for at in range(2)
            ]
            one = owner_parts(order, (), width, hidden, *halves, down[: rows_d // 2], down[rows_d // 2 :])
            found.append((*one, *triple_owner(order, (), width, *jnp.split(first, 2), last, jnp.zeros_like(last))))
        grad_expand, grad_reduce, grad_output, *early, grad_triple, g_1, s_1, q_1, v_1 = [list(one) for one in zip(*found)]
        late = [g_1, s_1, q_1, v_1]
        grad_expand, grad_reduce, grad_output, grad_triple = [
            scatter(jnp.concatenate(one).astype(BF)).astype(F32)
            for one in (grad_expand, grad_reduce, grad_output, grad_triple)
        ]

    def one_vector(*rows):
        if local:
            return jnp.concatenate([one.reshape(-1) for one in rows]) if len(rows) > 1 else rows[0].reshape(-1)
        whole = jnp.concatenate([one.reshape(-1) for parts in zip(*rows) for one in parts])
        return scatter(whole.astype(BF)).astype(F32)

    return (
        out_tokens,
        grad_tokens,
        one_vector(late[0]),
        one_vector(late[1]),
        grad_triple,
        one_vector(late[2], late[3]),
        grad_output,
        one_vector(early[2]),
        one_vector(early[0]),
        one_vector(early[1]),
        grad_expand,
        one_vector(early[4]),
        grad_reduce,
        one_vector(early[3]),
    )


def solution(mesh):
    return jax.shard_map(
        functools.partial(shards, mesh.shape["shard"]),
        mesh=mesh,
        in_specs=(
            P(("shard", "rep"), None),
            P(("shard", "rep")),
            P(("shard", "rep"), None),
            P("shard"),
            P("shard"),
            P("shard", None),
            P("shard"),
            P("shard", None),
            P("shard"),
            P("shard"),
            P("shard"),
            P("shard", None),
            P("shard"),
            P("shard", None),
            P("shard"),
        ),
        out_specs=(
            P(("shard", "rep"), None),
            P(("shard", "rep"), None),
            P("shard"),
            P("shard"),
            P("shard", None),
            P("shard"),
            P("shard", None),
            P("shard"),
            P("shard"),
            P("shard"),
            P("shard", None),
            P("shard"),
            P("shard", None),
            P("shard"),
        ),
        check_vma=False,
    )
```
